32 devices in a mesh: row: 8 (over z, x), col: 4 (over y, core).
Axes of the slice: x: 2, y: 2, z: 4, core: 2. Of those that a mesh axis runs over, the one named last changes fastest.
Arguments:
- volume: float32 [32, 128, 512], P('col', 'row'), may hold values from -4 to 4
Outputs:
- denoised: float32 [32, 128, 512], P('col', 'row')
- flux_x: float32 [32, 128, 512], P('col', 'row')
The draws below stay inside these ranges and needn't reach their ends.
All inputs are finite; a program needn't handle non-finite values.
Results may differ from the reference program's by a relative error of at most 0.00014.
Values sent between devices are 32-bit elements; how exact they have to be, the bound alone decides.
A program may use at most 64 MiB of HBM per device.

```python
import math
import jax
import jax.numpy as jnp

NX = 512
PASSES = 3
ITERS = 2
NY = 128
NZ = 32


def draw_volume(key, part):
    extent = (NZ, NY, NX)
    return jnp.clip(jax.random.normal(key, extent, jnp.float32), -4.0, 4.0)


def setup_inputs(seed: int = 0) -> dict:
    splits = jax.random.split(jax.random.key(seed), 2)
    volume = draw_volume(jax.random.fold_in(splits[1], 71), 0)
    return dict(volume=volume)


TIME_STEP = 0.16
EDGE_SCALE = 2.0
LOW_DIFFUSIVITY = 0.2
DIFFUSIVITY_SPAN = 1.8
GRAY_SLOPE = 2.5
REFERENCE_DIFFUSIVITY = 1.1


def diffuse(values):
    summed = jnp.zeros_like(values)
    for axis_number in range(3):
        for offset in (1, -1):
            differ = jnp.roll(values, offset, axis=axis_number) - values
            summed = summed + differ / (1.0 + (differ / EDGE_SCALE) ** 2)
    return values + TIME_STEP * summed


def green_multiplier():
    z_wave = jnp.arange(NZ, dtype=jnp.float32)[:, None, None]
    y_wave = jnp.arange(NY, dtype=jnp.float32)[None, :, None]
    x_wave = jnp.arange(NX // 2 + 1, dtype=jnp.float32)[None, None, :]
    spread = 4.0 * jnp.sin(math.pi * z_wave / NZ) ** 2 + 4.0 * jnp.sin(math.pi * y_wave / NY) ** 2 + 4.0 * jnp.sin(math.pi * x_wave / NX) ** 2
    zero_mode = (z_wave == 0) & (y_wave == 0) & (x_wave == 0)
    dropped = zero_mode | (x_wave == NX // 2)
    return jnp.where(dropped, 0.0, 1.0 / (REFERENCE_DIFFUSIVITY * jnp.where(zero_mode, 1.0, spread)))


def solve(diverge, multiplier):
    spectrum = jnp.fft.rfftn(diverge, axes=(0, 1, 2))
    return jnp.fft.irfftn(spectrum * multiplier, s=diverge.shape, axes=(0, 1, 2)).astype(jnp.float32)


def reference(volume):
    smooth = volume
    for sweep_index in range(PASSES):
        smooth = diffuse(smooth)
    diffusivity = LOW_DIFFUSIVITY + DIFFUSIVITY_SPAN * jax.nn.sigmoid(GRAY_SLOPE * smooth)
    excess = diffusivity - REFERENCE_DIFFUSIVITY
    multiplier = green_multiplier()
    potential = solve(excess - jnp.roll(excess, 1, axis=2), multiplier)
    for turn_index in range(ITERS - 1):
        tau_x = excess * (1.0 + jnp.roll(potential, -1, axis=2) - potential)
        tau_y = excess * (jnp.roll(potential, -1, axis=1) - potential)
        tau_z = excess * (jnp.roll(potential, -1, axis=0) - potential)
        diverge = (tau_x - jnp.roll(tau_x, 1, axis=2)) + (tau_y - jnp.roll(tau_y, 1, axis=1)) + (tau_z - jnp.roll(tau_z, 1, axis=0))
        potential = solve(diverge, multiplier)
    flux_x = diffusivity * (1.0 + jnp.roll(potential, -1, axis=2) - potential)
    return smooth, flux_x
```

```python
import functools
import math

import jax
import jax.numpy as jnp
import numpy as np
from jax import lax
from jax.experimental import pallas as pl
from jax.experimental.pallas import tpu as pltpu
from jax.sharding import PartitionSpec as P

PASSES = 3


HIGHEST = lax.Precision.HIGHEST
TIME_STEP = 0.16
EDGE_SCALE = 2.0
LOW_DIFFUSIVITY = 0.2
DIFFUSIVITY_SPAN = 1.8
GRAY_SLOPE = 2.5
REFERENCE_DIFFUSIVITY = 1.1


def with_halo(block, sides, width):
    for axis, dim in sides:
        count = lax.axis_size(axis)
        forward = [(i, i + 1) for i in range(count - 1)]
        forward.append((count - 1, 0))
        backward = [(target, source) for source, target in forward]
        low = lax.ppermute(
            lax.slice_in_dim(block, block.shape[dim] - width, None, axis=dim), axis, forward
        )
        high = lax.ppermute(lax.slice_in_dim(block, 0, width, axis=dim), axis, backward)
        block = jnp.concatenate([low, block, high], axis=dim)
    return block


def diffuse(padded):
    center = padded[1:-1, 1:-1, :]
    summed = jnp.zeros_like(center)
    neighbours = (
        padded[:-2, 1:-1, :],
        padded[2:, 1:-1, :],
        padded[1:-1, :-2, :],
        padded[1:-1, 2:, :],
        jnp.roll(center, 1, axis=2),
        jnp.roll(center, -1, axis=2),
    )
    for member in neighbours:
        differ = member - center
        summed = summed + differ / (1.0 + (differ / EDGE_SCALE) ** 2)
    return center + TIME_STEP * summed


def phase_of(integers, length):
    return (integers % length).astype(jnp.float32) * (2.0 * math.pi / length)


def dft_table(length):
    counter = jnp.arange(length, dtype=jnp.int32)
    angles = phase_of(counter[:, None] * counter[None, :], length)
    return (jnp.cos(angles), jnp.sin(angles))


def plane_table(z_cells, y_cells, along_z):
    counter = jnp.arange(z_cells * y_cells, dtype=jnp.int32)
    z_place = counter // y_cells
    y_place = counter % y_cells
    if along_z:
        same = y_place[:, None] == y_place[None, :]
        angles = phase_of(z_place[:, None] * z_place[None, :], z_cells)
    else:
        same = z_place[:, None] == z_place[None, :]
        angles = phase_of(y_place[:, None] * y_place[None, :], y_cells)
    return (jnp.where(same, jnp.cos(angles), 0.0), jnp.where(same, jnp.sin(angles), 0.0))


def contract(pieces, tables, pattern, orient):
    real_part, imag_part = pieces
    cosine, sine_part = tables
    real_cos = jnp.einsum(pattern, real_part, cosine, precision=HIGHEST)
    imag_sin = jnp.einsum(pattern, imag_part, sine_part, precision=HIGHEST)
    imag_cos = jnp.einsum(pattern, imag_part, cosine, precision=HIGHEST)
    real_sin = jnp.einsum(pattern, real_part, sine_part, precision=HIGHEST)
    return (real_cos - orient * imag_sin, imag_cos + orient * real_sin)


def rotate(pieces, angles, orient):
    cosine = jnp.cos(angles)
    sine_part = jnp.sin(angles)
    real_part, imag_part = pieces
    return (
        real_part * cosine - orient * imag_part * sine_part,
        imag_part * cosine + orient * real_part * sine_part,
    )


def y_twiddle(row_count, z_cells, y_cells):
    within = jnp.arange(z_cells * y_cells, dtype=jnp.int32) % y_cells
    orders = jnp.arange(row_count, dtype=jnp.int32)
    return phase_of(orders[:, None] * within[None, :], row_count * y_cells)[:, None, :]


def z_twiddle(col_count, z_cells, y_cells):
    within = jnp.arange(z_cells * y_cells, dtype=jnp.int32) // y_cells
    orders = jnp.arange(col_count, dtype=jnp.int32)
    return phase_of(orders[:, None] * within[None, :], col_count * z_cells)[:, None, None, :]


def row_transpose(pieces):
    return (
        lax.all_to_all(pieces[0], "row", split_axis=1, concat_axis=1, tiled=True),
        lax.all_to_all(pieces[1], "row", split_axis=1, concat_axis=1, tiled=True),
    )


def col_transpose(pieces):
    return (
        lax.all_to_all(pieces[0], "col", split_axis=1, concat_axis=1, tiled=True),
        lax.all_to_all(pieces[1], "col", split_axis=1, concat_axis=1, tiled=True),
    )


def reshape_all(pieces, extent):
    return (pieces[0].reshape(extent), pieces[1].reshape(extent))


def forward(source):
    fields, z_cells, y_cells, x_cells = source.shape
    row_count = lax.axis_size("row")
    col_count = lax.axis_size("col")
    half_width = x_cells // 2
    per_row = half_width // row_count
    block_share = row_count // col_count
    plane_cells = z_cells * y_cells
    flat = source.reshape(fields, plane_cells, x_cells)
    x_index = jnp.arange(x_cells, dtype=jnp.int32)
    k_index = jnp.arange(half_width, dtype=jnp.int32)
    angles = phase_of(x_index[:, None] * k_index[None, :], x_cells)
    real_part = jnp.einsum("fmx,xk->fkm", flat, jnp.cos(angles), precision=HIGHEST)
    imag_part = -jnp.einsum("fmx,xk->fkm", flat, jnp.sin(angles), precision=HIGHEST)
    pieces = reshape_all((real_part, imag_part), (fields, row_count, per_row, plane_cells))
    pieces = row_transpose(pieces)
    pieces = contract(pieces, dft_table(row_count), "fskm,sp->fpkm", -1.0)
    pieces = rotate(pieces, y_twiddle(row_count, z_cells, y_cells), -1.0)
    pieces = contract(pieces, plane_table(z_cells, y_cells, False), "fpkm,mn->fpkn", -1.0)
    pieces = reshape_all(pieces, (fields, col_count, block_share * per_row * plane_cells))
    pieces = col_transpose(pieces)
    pieces = reshape_all(pieces, (fields, col_count, block_share, per_row, plane_cells))
    pieces = contract(pieces, dft_table(col_count), "fcabm,cp->fpabm", -1.0)
    pieces = rotate(pieces, z_twiddle(col_count, z_cells, y_cells), -1.0)
    return contract(pieces, plane_table(z_cells, y_cells, True), "fpabm,mn->fpabn", -1.0)


def inverse(pieces, z_cells, y_cells, x_cells):
    fields, col_count, block_share, per_row, plane_cells = pieces[0].shape
    row_count = col_count * block_share
    half_width = row_count * per_row
    pieces = contract(pieces, plane_table(z_cells, y_cells, True), "fpabn,nm->fpabm", 1.0)
    pieces = rotate(pieces, z_twiddle(col_count, z_cells, y_cells), 1.0)
    pieces = contract(pieces, dft_table(col_count), "fpabm,pc->fcabm", 1.0)
    pieces = reshape_all(pieces, (fields, col_count, block_share * per_row * plane_cells))
    pieces = col_transpose(pieces)
    pieces = reshape_all(pieces, (fields, row_count, per_row, plane_cells))
    pieces = contract(pieces, plane_table(z_cells, y_cells, False), "fpkn,nm->fpkm", 1.0)
    pieces = rotate(pieces, y_twiddle(row_count, z_cells, y_cells), 1.0)
    pieces = contract(pieces, dft_table(row_count), "fpkm,ps->fskm", 1.0)
    pieces = row_transpose(pieces)
    pieces = reshape_all(pieces, (fields, half_width, plane_cells))
    k_index = jnp.arange(half_width, dtype=jnp.int32)
    x_index = jnp.arange(x_cells, dtype=jnp.int32)
    angles = phase_of(k_index[:, None] * x_index[None, :], x_cells)
    weight = jnp.where(k_index == 0, 1.0, 2.0).astype(jnp.float32)[:, None]
    real_out = jnp.einsum("fkm,kx->fmx", pieces[0], weight * jnp.cos(angles), precision=HIGHEST)
    imag_out = jnp.einsum("fkm,kx->fmx", pieces[1], weight * jnp.sin(angles), precision=HIGHEST)
    return (real_out - imag_out).reshape(fields, z_cells, y_cells, x_cells)


def spectral_tables(z_cells, y_cells, x_cells):
    row_count = lax.axis_size("row")
    col_count = lax.axis_size("col")
    block_share = row_count // col_count
    per_row = x_cells // 2 // row_count
    plane = jnp.arange(z_cells * y_cells, dtype=jnp.int32)
    z_wave = (
        jnp.arange(col_count, dtype=jnp.int32)[:, None, None, None]
        + col_count * (plane // y_cells)[None, None, None, :]
    )
    y_wave = (lax.axis_index("col") * block_share + jnp.arange(block_share, dtype=jnp.int32))[
        None, :, None, None
    ] + row_count * (plane % y_cells)[None, None, None, :]
    x_wave = (lax.axis_index("row") * per_row + jnp.arange(per_row, dtype=jnp.int32))[
        None, None, :, None
    ]
    k_extent = (col_count, block_share, per_row, z_cells * y_cells)
    angle_list = [
        jnp.broadcast_to(member, k_extent)
        for member in (
            phase_of(x_wave, x_cells),
            phase_of(y_wave, row_count * y_cells),
            phase_of(z_wave, col_count * z_cells),
        )
    ]
    plus_symbols = [(jnp.cos(member) - 1.0, jnp.sin(member)) for member in angle_list]
    minus_symbols = [(1.0 - jnp.cos(member), jnp.sin(member)) for member in angle_list]
    spread = (
        4.0 * jnp.sin(0.5 * angle_list[0]) ** 2
        + 4.0 * jnp.sin(0.5 * angle_list[1]) ** 2
        + 4.0 * jnp.sin(0.5 * angle_list[2]) ** 2
    )
    zero_mode = (x_wave == 0) & (y_wave == 0) & (z_wave == 0)
    total_cells = float(x_cells * row_count * y_cells * col_count * z_cells)
    multiplier = jnp.where(
        zero_mode,
        0.0,
        1.0 / (REFERENCE_DIFFUSIVITY * jnp.where(zero_mode, 1.0, spread) * total_cells),
    )
    return (plus_symbols, minus_symbols, multiplier)


def times_symbol(symbol, pieces):
    symbol_real, symbol_imag = symbol
    return (
        symbol_real * pieces[0] - symbol_imag * pieces[1],
        symbol_real * pieces[1] + symbol_imag * pieces[0],
    )


def stack_symbols(symbols, pieces):
    products = [times_symbol(symbol, pieces) for symbol in symbols]
    return (
        jnp.concatenate([member[0] for member in products], axis=0),
        jnp.concatenate([member[1] for member in products], axis=0),
    )


def contract_symbols(symbols, pieces):
    real_sum = jnp.zeros_like(pieces[0][0:1])
    imag_sum = jnp.zeros_like(pieces[1][0:1])
    for direction in range(3):
        product = times_symbol(
            symbols[direction],
            (pieces[0][direction : direction + 1], pieces[1][direction : direction + 1]),
        )
        real_sum = real_sum + product[0]
        imag_sum = imag_sum + product[1]
    return (real_sum, imag_sum)


def rescale(multiplier, pieces):
    return (multiplier * pieces[0], multiplier * pieces[1])


def on_device_general(volume):
    z_cells, y_cells, x_cells = volume.shape
    smooth = volume
    for sweep_index in range(PASSES):
        padded = with_halo(smooth, (("row", 1), ("col", 0)), 1)
        smooth = diffuse(padded)
    diffusivity = LOW_DIFFUSIVITY + DIFFUSIVITY_SPAN * jax.nn.sigmoid(GRAY_SLOPE * smooth)
    excess = diffusivity - REFERENCE_DIFFUSIVITY
    plus_symbols, minus_symbols, multiplier = spectral_tables(z_cells, y_cells, x_cells)
    source = (excess - jnp.roll(excess, 1, axis=2))[None]
    potential_hat = rescale(multiplier, forward(source))
    unit_load = jnp.array([1.0, 0.0, 0.0], jnp.float32)[:, None, None, None]
    gradients = inverse(stack_symbols(plus_symbols, potential_hat), z_cells, y_cells, x_cells)
    tau_hat = forward(excess[None] * (gradients + unit_load))
    potential_hat = rescale(multiplier, contract_symbols(minus_symbols, tau_hat))
    gradient_x = inverse(times_symbol(plus_symbols[0], potential_hat), z_cells, y_cells, x_cells)[0]
    flux_x = diffusivity * (1.0 + gradient_x)
    return (smooth, flux_x)


MESH = pl.DeviceIdType.MESH
NT = (((1,), (1,)), ((), ()))
NN = (((1,), (0,)), ((), ()))
LANES = 128
SUBLANES = 8
EXCHANGES = PASSES + 1


def split(values):
    high = values.astype(jnp.bfloat16)
    return high, (values - high.astype(jnp.float32)).astype(jnp.bfloat16)


def split_numpy(values):
    high = values.astype(np.float32).astype(jnp.bfloat16)
    return high, (values - high.astype(np.float64)).astype(np.float32).astype(jnp.bfloat16)


def host_tables(rows, cols, z_cells, y_cells, x_cells):
    devices = rows * cols
    half = x_cells // 2
    k = np.arange(half)
    turn = 2.0 * np.pi * ((k[:, None] * np.arange(x_cells)[None, :]) % x_cells) / x_cells
    wave = np.stack([np.cos(turn), -np.sin(turn)])
    wave = wave.reshape(2, devices, SUBLANES, x_cells).transpose(1, 0, 2, 3)
    wave = wave.reshape(2 * half, x_cells)
    zl, yl = np.divmod(np.arange(LANES), y_cells)
    c, r = np.divmod(np.arange(devices), rows)
    inner = 2.0 * np.pi * (zl[:, None] * zl[None, :] / z_cells + yl[:, None] * yl[None, :] / y_cells)
    cosine, sine = np.cos(inner), np.sin(inner)
    plane = np.block([[cosine, -sine], [sine, cosine]])
    nz, ny = cols * z_cells, rows * y_cells
    twist = 2.0 * np.pi * (c[:, None] * zl[None, :] / nz + r[:, None] * yl[None, :] / ny)
    kz = c[:, None] + cols * zl[None, :]
    ky = r[:, None] + rows * yl[None, :]
    lam_zy = 4.0 * np.sin(np.pi * kz / nz) ** 2 + 4.0 * np.sin(np.pi * ky / ny) ** 2
    lam_x = (4.0 * np.sin(np.pi * k / x_cells) ** 2).reshape(devices, SUBLANES, 1)
    weight = np.where(k == 0, 1.0, 2.0) / (REFERENCE_DIFFUSIVITY * nz * ny * x_cells)
    weight = weight.reshape(devices, SUBLANES, 1)
    shape = (devices, SUBLANES, LANES)
    small = np.stack(
        [
            np.broadcast_to(np.cos(twist)[:, None, :], shape),
            np.broadcast_to(np.sin(twist)[:, None, :], shape),
            np.broadcast_to(lam_zy[:, None, :], shape),
            np.broadcast_to(lam_x, shape),
            np.broadcast_to(weight, shape),
        ]
    ).astype(np.float32)
    return split_numpy(wave) + split_numpy(plane) + (small,)


def small_fft(items, sign):
    size = len(items)
    if size == 1:
        return items
    even, odd = small_fft(items[::2], sign), small_fft(items[1::2], sign)
    low, high = [], []
    for k in range(size // 2):
        (er, ei), (xr, xi) = even[k], odd[k]
        if 4 * k == size:
            xr, xi = -sign * xi, sign * xr
        elif k:
            co, si = math.cos(2 * math.pi * k / size), sign * math.sin(2 * math.pi * k / size)
            xr, xi = xr * co - xi * si, xr * si + xi * co
        low.append((er + xr, ei + xi))
        high.append((er - xr, ei - xi))
    return low + high


def grid_fft(items, rows, cols, sign):
    lines = [small_fft(items[c * rows : (c + 1) * rows], sign) for c in range(cols)]
    columns = [small_fft([lines[c][r] for c in range(cols)], sign) for r in range(rows)]
    return [columns[r][c] for c in range(cols) for r in range(rows)]


def kernel(
    rows, cols, z_cells, y_cells, x_cells,
    volume, wave_hi_hbm, wave_lo_hbm, plane_hi_hbm, plane_lo_hbm, small_hbm,
    smooth_out, flux_out,
    wave_hi, wave_lo, plane_hi, plane_lo, small,
    field, excess_ref, y_send, y_recv, z_recv, ey_send, ey_recv, ez_recv,
    packed, arrived,
    table_sem, halo_send, halo_recv, e_send, e_recv, all_send, all_recv,
):
    devices = rows * cols
    cells = z_cells * y_cells
    row, col = lax.axis_index("row"), lax.axis_index("col")
    me = col * rows + row
    up_row, down_row = lax.rem(row + 1, rows), lax.rem(row + rows - 1, rows)
    up_col, down_col = lax.rem(col + 1, cols), lax.rem(col + cols - 1, cols)

    loads = [
        pltpu.make_async_copy(source, target, table_sem.at[i])
        for i, (source, target) in enumerate(
            (
                (wave_hi_hbm, wave_hi), (wave_lo_hbm, wave_lo), (plane_hi_hbm, plane_hi),
                (plane_lo_hbm, plane_lo), (small_hbm, small),
            )
        )
    ]
    for load in loads:
        load.start()

    barrier = pltpu.get_barrier_semaphore()

    def greet(step, carry):
        other = lax.rem(me + step, devices)
        pl.semaphore_signal(
            barrier, inc=1, device_id=(lax.rem(other, rows), other // rows), device_id_type=MESH
        )
        return carry

    lax.fori_loop(1, devices, greet, 0)
    pl.semaphore_wait(barrier, devices - 1)

    place = lax.broadcasted_iota(jnp.int32, (cells, x_cells), 0)
    first_y = lax.rem(place, y_cells) == 0
    last_y = lax.rem(place, y_cells) == y_cells - 1

    def spread(edge):
        wide = jnp.broadcast_to(edge[:, None, :], (z_cells, y_cells, x_cells))
        return wide.reshape(cells, x_cells)

    def edge_of(values, y):
        return values.reshape(z_cells, y_cells, x_cells)[:, y, :]

    def remote(source, target, send, recv, device):
        return pltpu.make_async_remote_copy(
            src_ref=source, dst_ref=target, send_sem=send, recv_sem=recv,
            device_id=device, device_id_type=MESH,
        )

    def start_halo(e):
        y_send[e, 0] = edge_of(field[e], y_cells - 1)
        y_send[e, 1] = edge_of(field[e], 0)
        copies = (
            remote(y_send.at[e, 0], y_recv.at[e, 0], halo_send.at[e, 0], halo_recv.at[e, 0], (up_row, col)),
            remote(y_send.at[e, 1], y_recv.at[e, 1], halo_send.at[e, 1], halo_recv.at[e, 1], (down_row, col)),
            remote(field.at[e, pl.ds(cells - y_cells, y_cells)], z_recv.at[e, 0],
                   halo_send.at[e, 2], halo_recv.at[e, 2], (row, up_col)),
            remote(field.at[e, pl.ds(0, y_cells)], z_recv.at[e, 1],
                   halo_send.at[e, 3], halo_recv.at[e, 3], (row, down_col)),
        )
        for copy in copies:
            copy.start()
        return copies

    def next_x(v):
        return pltpu.roll(v, x_cells - 1, 1)

    def prev_x(v):
        return pltpu.roll(v, 1, 1)

    def limited(differ):
        scaled = differ / EDGE_SCALE
        return differ / (1.0 + scaled * scaled)

    pending = []
    field[0] = volume[...].reshape(cells, x_cells)
    for sweep in range(PASSES):
        copies = start_halo(sweep)
        pending += copies
        now = field[sweep]
        flow = limited(next_x(now) - now)
        total = flow - prev_x(flow)
        inner_z = limited(now[y_cells:] - now[:-y_cells])
        for copy in copies:
            copy.wait_recv()
        above = jnp.where(last_y, spread(y_recv[sweep, 1]), pltpu.roll(now, cells - 1, 0))
        flow = limited(above - now)
        edge = limited(edge_of(now, 0) - y_recv[sweep, 0])
        total = total + (flow - jnp.where(first_y, spread(edge), pltpu.roll(flow, 1, 0)))
        z_low = limited(now[:y_cells] - z_recv[sweep, 0])
        z_high = limited(z_recv[sweep, 1] - now[-y_cells:])
        total = total + (
            jnp.concatenate([inner_z, z_high], axis=0) - jnp.concatenate([z_low, inner_z], axis=0)
        )
        later = now + TIME_STEP * total
        if sweep < PASSES - 1:
            field[sweep + 1] = later
    smooth_out[...] = later.reshape(z_cells, y_cells, x_cells)
    diffusivity = LOW_DIFFUSIVITY + DIFFUSIVITY_SPAN / (1.0 + jnp.exp(-GRAY_SLOPE * later))
    flux_out[...] = diffusivity.reshape(z_cells, y_cells, x_cells)
    excess = diffusivity - REFERENCE_DIFFUSIVITY
    excess_ref[...] = excess
    ey_send[...] = edge_of(excess, y_cells - 1)
    e_copies = (
        remote(ey_send, ey_recv, e_send.at[0], e_recv.at[0], (up_row, col)),
        remote(excess_ref.at[pl.ds(cells - y_cells, y_cells)], ez_recv, e_send.at[1], e_recv.at[1], (row, up_col)),
    )
    for copy in e_copies:
        copy.start()
    pending += e_copies
    for load in loads:
        load.wait()

    def exchange(turn):
        def send(step, carry):
            other = lax.rem(me + step, devices)
            remote(
                packed.at[turn, other], arrived.at[turn, me], all_send.at[turn], all_recv.at[turn],
                (lax.rem(other, rows), other // rows),
            ).start()
            return carry

        lax.fori_loop(1, devices, send, 0)
        arrived[turn, me] = packed[turn, me]
        block = arrived.at[turn, pl.ds(0, devices - 1)]
        pltpu.make_async_copy(block, block, all_recv.at[turn]).wait()

    def finish(turn):
        block = packed.at[turn, pl.ds(0, devices - 1)]
        pltpu.make_async_copy(block, block, all_send.at[turn]).wait()

    def product(a, b, dims):
        return lax.dot_general(a, b, dims, preferred_element_type=jnp.float32)

    def row_product(values, high, low, dims):
        values_hi, values_lo = split(values)
        count = values.shape[0]
        both = product(jnp.concatenate([values_hi, values_lo], axis=0), high, dims)
        return both[:count] + (both[count:] + product(values_hi, low, dims))

    def solve(source, turn):
        source_hi, source_lo = split(source)
        both = product(wave_hi[...], jnp.concatenate([source_hi, source_lo], axis=0), NT)
        spectrum = both[:, :cells] + (both[:, cells:] + product(wave_lo[...], source_hi, NT))
        packed[turn] = spectrum.reshape(devices, 2 * SUBLANES, LANES)
        exchange(turn)
        items = [(arrived[turn, d, :SUBLANES], arrived[turn, d, SUBLANES:]) for d in range(devices)]
        items = grid_fft(items, rows, cols, -1.0)
        turned = []
        for d, (re, im) in enumerate(items):
            co, si = small[0, d], small[1, d]
            turned.append(jnp.concatenate([re * co + im * si, im * co - re * si], axis=1))
        waves = row_product(jnp.concatenate(turned, axis=0), plane_hi[...], plane_lo[...], NN)
        lam = small[2] + small[3, me][None]
        factor = jnp.where(lam == 0.0, 0.0, small[4, me][None] / jnp.where(lam == 0.0, 1.0, lam))
        factor = factor.reshape(devices * SUBLANES, LANES)
        waves = waves * jnp.concatenate([factor, factor], axis=1)
        waves = row_product(waves, plane_hi[...], plane_lo[...], NT)
        items = []
        for d in range(devices):
            part = waves[d * SUBLANES : (d + 1) * SUBLANES]
            re, im = part[:, :LANES], part[:, LANES:]
            co, si = small[0, d], small[1, d]
            items.append((re * co - im * si, im * co + re * si))
        items = grid_fft(items, rows, cols, 1.0)
        for d, (re, im) in enumerate(items):
            packed[turn + 1, d, :SUBLANES] = re
            packed[turn + 1, d, SUBLANES:] = im
        exchange(turn + 1)
        back = arrived[turn + 1].reshape(2 * SUBLANES * devices, LANES)
        return row_product(back.T, wave_hi[...], wave_lo[...], NN)

    potential = solve(excess - prev_x(excess), 0)
    field[PASSES] = potential
    copies = start_halo(PASSES)
    pending += copies
    potential = field[PASSES]
    excess = excess_ref[...]
    tau = excess * (1.0 + (next_x(potential) - potential))
    diverge = tau - prev_x(tau)
    inner_z = excess[:-y_cells] * (potential[y_cells:] - potential[:-y_cells])
    for copy in e_copies + copies:
        copy.wait_recv()
    above = jnp.where(last_y, spread(y_recv[PASSES, 1]), pltpu.roll(potential, cells - 1, 0))
    tau = excess * (above - potential)
    edge = ey_recv[...] * (edge_of(potential, 0) - y_recv[PASSES, 0])
    diverge = diverge + (tau - jnp.where(first_y, spread(edge), pltpu.roll(tau, 1, 0)))
    z_low = ez_recv[...] * (potential[:y_cells] - z_recv[PASSES, 0])
    z_high = excess[-y_cells:] * (z_recv[PASSES, 1] - potential[-y_cells:])
    diverge = diverge + (
        jnp.concatenate([inner_z, z_high], axis=0) - jnp.concatenate([z_low, inner_z], axis=0)
    )
    potential = solve(diverge, 2)
    gradient = next_x(potential) - potential
    flux_out[...] = flux_out[...] * (1.0 + gradient.reshape(z_cells, y_cells, x_cells))
    for copy in pending:
        copy.wait_send()
    for turn in range(4):
        finish(turn)


def on_device(rows, cols, tables, volume):
    z_cells, y_cells, x_cells = volume.shape
    devices, cells = rows * cols, z_cells * y_cells
    f32, bf16 = jnp.float32, jnp.bfloat16
    vmem = pl.BlockSpec(memory_space=pltpu.VMEM)
    scratch = [pltpu.VMEM(table.shape, table.dtype) for table in tables] + [
        pltpu.VMEM((EXCHANGES, cells, x_cells), f32),
        pltpu.VMEM((cells, x_cells), f32),
        pltpu.VMEM((EXCHANGES, 2, z_cells, x_cells), f32),
        pltpu.VMEM((EXCHANGES, 2, z_cells, x_cells), f32),
        pltpu.VMEM((EXCHANGES, 2, y_cells, x_cells), f32),
        pltpu.VMEM((z_cells, x_cells), f32),
        pltpu.VMEM((z_cells, x_cells), f32),
        pltpu.VMEM((y_cells, x_cells), f32),
        pltpu.VMEM((4, devices, 2 * SUBLANES, LANES), f32),
        pltpu.VMEM((4, devices, 2 * SUBLANES, LANES), f32),
        pltpu.SemaphoreType.DMA((len(tables),)),
        pltpu.SemaphoreType.DMA((EXCHANGES, 4)),
        pltpu.SemaphoreType.DMA((EXCHANGES, 4)),
        pltpu.SemaphoreType.DMA((2,)),
        pltpu.SemaphoreType.DMA((2,)),
        pltpu.SemaphoreType.DMA((4,)),
        pltpu.SemaphoreType.DMA((4,)),
    ]
    shape = jax.ShapeDtypeStruct(volume.shape, f32)
    return pl.pallas_call(
        functools.partial(kernel, rows, cols, z_cells, y_cells, x_cells),
        out_shape=(shape, shape),
        in_specs=[vmem] + [pl.BlockSpec(memory_space=pl.ANY)] * len(tables),
        out_specs=(vmem, vmem),
        scratch_shapes=scratch,
        compiler_params=pltpu.CompilerParams(
            collective_id=0, has_side_effects=True, vmem_limit_bytes=32 * 1024 * 1024
        ),
    )(volume, *tables)


def power_of_two(count):
    return count & (count - 1) == 0


def block_function(rows, cols, volume):
    z_cells, y_cells, x_cells = volume.shape
    devices = rows * cols
    direct = (
        x_cells // 2 == SUBLANES * devices
        and z_cells * y_cells == LANES
        and z_cells % 8 == 0
        and y_cells % 8 == 0
        and power_of_two(rows)
        and power_of_two(cols)
        and min(rows, cols) > 2
    )
    if not direct:
        return on_device_general(volume)
    tables = [jnp.asarray(t) for t in host_tables(rows, cols, z_cells, y_cells, x_cells)]
    return on_device(rows, cols, tables, volume)


def solution(mesh):
    return jax.shard_map(
        functools.partial(block_function, mesh.shape["row"], mesh.shape["col"]),
        mesh=mesh,
        in_specs=(P("col", "row", None),),
        out_specs=(P("col", "row", None), P("col", "row", None)),
        check_vma=False,
    )
```

```python
import functools
import math

import jax
import jax.numpy as jnp
import numpy as np
from jax import lax
from jax.experimental import pallas as pl
from jax.experimental.pallas import tpu as pltpu
from jax.sharding import PartitionSpec as P

PASSES = 3


HIGHEST = lax.Precision.HIGHEST
TIME_STEP = 0.16
EDGE_SCALE = 2.0
LOW_DIFFUSIVITY = 0.2
DIFFUSIVITY_SPAN = 1.8
GRAY_SLOPE = 2.5
REFERENCE_DIFFUSIVITY = 1.1


def with_halo(block, sides, width):
    for axis, dim in sides:
        count = lax.axis_size(axis)
        forward = [(i, i + 1) for i in range(count - 1)]
        forward.append((count - 1, 0))
        backward = [(target, source) for source, target in forward]
        low = lax.ppermute(
            lax.slice_in_dim(block, block.shape[dim] - width, None, axis=dim), axis, forward
        )
        high = lax.ppermute(lax.slice_in_dim(block, 0, width, axis=dim), axis, backward)
        block = jnp.concatenate([low, block, high], axis=dim)
    return block


def diffuse(padded):
    center = padded[1:-1, 1:-1, :]
    summed = jnp.zeros_like(center)
    neighbours = (
        padded[:-2, 1:-1, :],
        padded[2:, 1:-1, :],
        padded[1:-1, :-2, :],
        padded[1:-1, 2:, :],
        jnp.roll(center, 1, axis=2),
        jnp.roll(center, -1, axis=2),
    )
    for member in neighbours:
        differ = member - center
        summed = summed + differ / (1.0 + (differ / EDGE_SCALE) ** 2)
    return center + TIME_STEP * summed


def phase_of(integers, length):
    return (integers % length).astype(jnp.float32) * (2.0 * math.pi / length)


def dft_table(length):
    counter = jnp.arange(length, dtype=jnp.int32)
    angles = phase_of(counter[:, None] * counter[None, :], length)
    return (jnp.cos(angles), jnp.sin(angles))


def plane_table(z_cells, y_cells, along_z):
    counter = jnp.arange(z_cells * y_cells, dtype=jnp.int32)
    z_place = counter // y_cells
    y_place = counter % y_cells
    if along_z:
        same = y_place[:, None] == y_place[None, :]
        angles = phase_of(z_place[:, None] * z_place[None, :], z_cells)
    else:
        same = z_place[:, None] == z_place[None, :]
        angles = phase_of(y_place[:, None] * y_place[None, :], y_cells)
    return (jnp.where(same, jnp.cos(angles), 0.0), jnp.where(same, jnp.sin(angles), 0.0))


def contract(pieces, tables, pattern, orient):
    real_part, imag_part = pieces
    cosine, sine_part = tables
    real_cos = jnp.einsum(pattern, real_part, cosine, precision=HIGHEST)
    imag_sin = jnp.einsum(pattern, imag_part, sine_part, precision=HIGHEST)
    imag_cos = jnp.einsum(pattern, imag_part, cosine, precision=HIGHEST)
    real_sin = jnp.einsum(pattern, real_part, sine_part, precision=HIGHEST)
    return (real_cos - orient * imag_sin, imag_cos + orient * real_sin)


def rotate(pieces, angles, orient):
    cosine = jnp.cos(angles)
    sine_part = jnp.sin(angles)
    real_part, imag_part = pieces
    return (
        real_part * cosine - orient * imag_part * sine_part,
        imag_part * cosine + orient * real_part * sine_part,
    )


def y_twiddle(row_count, z_cells, y_cells):
    within = jnp.arange(z_cells * y_cells, dtype=jnp.int32) % y_cells
    orders = jnp.arange(row_count, dtype=jnp.int32)
    return phase_of(orders[:, None] * within[None, :], row_count * y_cells)[:, None, :]


def z_twiddle(col_count, z_cells, y_cells):
    within = jnp.arange(z_cells * y_cells, dtype=jnp.int32) // y_cells
    orders = jnp.arange(col_count, dtype=jnp.int32)
    return phase_of(orders[:, None] * within[None, :], col_count * z_cells)[:, None, None, :]


def row_transpose(pieces):
    return (
        lax.all_to_all(pieces[0], "row", split_axis=1, concat_axis=1, tiled=True),
        lax.all_to_all(pieces[1], "row", split_axis=1, concat_axis=1, tiled=True),
    )


def col_transpose(pieces):
    return (
        lax.all_to_all(pieces[0], "col", split_axis=1, concat_axis=1, tiled=True),
        lax.all_to_all(pieces[1], "col", split_axis=1, concat_axis=1, tiled=True),
    )


def reshape_all(pieces, extent):
    return (pieces[0].reshape(extent), pieces[1].reshape(extent))


def forward(source):
    fields, z_cells, y_cells, x_cells = source.shape
    row_count = lax.axis_size("row")
    col_count = lax.axis_size("col")
    half_width = x_cells // 2
    per_row = half_width // row_count
    block_share = row_count // col_count
    plane_cells = z_cells * y_cells
    flat = source.reshape(fields, plane_cells, x_cells)
    x_index = jnp.arange(x_cells, dtype=jnp.int32)
    k_index = jnp.arange(half_width, dtype=jnp.int32)
    angles = phase_of(x_index[:, None] * k_index[None, :], x_cells)
    real_part = jnp.einsum("fmx,xk->fkm", flat, jnp.cos(angles), precision=HIGHEST)
    imag_part = -jnp.einsum("fmx,xk->fkm", flat, jnp.sin(angles), precision=HIGHEST)
    pieces = reshape_all((real_part, imag_part), (fields, row_count, per_row, plane_cells))
    pieces = row_transpose(pieces)
    pieces = contract(pieces, dft_table(row_count), "fskm,sp->fpkm", -1.0)
    pieces = rotate(pieces, y_twiddle(row_count, z_cells, y_cells), -1.0)
    pieces = contract(pieces, plane_table(z_cells, y_cells, False), "fpkm,mn->fpkn", -1.0)
    pieces = reshape_all(pieces, (fields, col_count, block_share * per_row * plane_cells))
    pieces = col_transpose(pieces)
    pieces = reshape_all(pieces, (fields, col_count, block_share, per_row, plane_cells))
    pieces = contract(pieces, dft_table(col_count), "fcabm,cp->fpabm", -1.0)
    pieces = rotate(pieces, z_twiddle(col_count, z_cells, y_cells), -1.0)
    return contract(pieces, plane_table(z_cells, y_cells, True), "fpabm,mn->fpabn", -1.0)


def inverse(pieces, z_cells, y_cells, x_cells):
    fields, col_count, block_share, per_row, plane_cells = pieces[0].shape
    row_count = col_count * block_share
    half_width = row_count * per_row
    pieces = contract(pieces, plane_table(z_cells, y_cells, True), "fpabn,nm->fpabm", 1.0)
    pieces = rotate(pieces, z_twiddle(col_count, z_cells, y_cells), 1.0)
    pieces = contract(pieces, dft_table(col_count), "fpabm,pc->fcabm", 1.0)
    pieces = reshape_all(pieces, (fields, col_count, block_share * per_row * plane_cells))
    pieces = col_transpose(pieces)
    pieces = reshape_all(pieces, (fields, row_count, per_row, plane_cells))
    pieces = contract(pieces, plane_table(z_cells, y_cells, False), "fpkn,nm->fpkm", 1.0)
    pieces = rotate(pieces, y_twiddle(row_count, z_cells, y_cells), 1.0)
    pieces = contract(pieces, dft_table(row_count), "fpkm,ps->fskm", 1.0)
    pieces = row_transpose(pieces)
    pieces = reshape_all(pieces, (fields, half_width, plane_cells))
    k_index = jnp.arange(half_width, dtype=jnp.int32)
    x_index = jnp.arange(x_cells, dtype=jnp.int32)
    angles = phase_of(k_index[:, None] * x_index[None, :], x_cells)
    weight = jnp.where(k_index == 0, 1.0, 2.0).astype(jnp.float32)[:, None]
    real_out = jnp.einsum("fkm,kx->fmx", pieces[0], weight * jnp.cos(angles), precision=HIGHEST)
    imag_out = jnp.einsum("fkm,kx->fmx", pieces[1], weight * jnp.sin(angles), precision=HIGHEST)
    return (real_out - imag_out).reshape(fields, z_cells, y_cells, x_cells)


def spectral_tables(z_cells, y_cells, x_cells):
    row_count = lax.axis_size("row")
    col_count = lax.axis_size("col")
    block_share = row_count // col_count
    per_row = x_cells // 2 // row_count
    plane = jnp.arange(z_cells * y_cells, dtype=jnp.int32)
    z_wave = (
        jnp.arange(col_count, dtype=jnp.int32)[:, None, None, None]
        + col_count * (plane // y_cells)[None, None, None, :]
    )
    y_wave = (lax.axis_index("col") * block_share + jnp.arange(block_share, dtype=jnp.int32))[
        None, :, None, None
    ] + row_count * (plane % y_cells)[None, None, None, :]
    x_wave = (lax.axis_index("row") * per_row + jnp.arange(per_row, dtype=jnp.int32))[
        None, None, :, None
    ]
    k_extent = (col_count, block_share, per_row, z_cells * y_cells)
    angle_list = [
        jnp.broadcast_to(member, k_extent)
        for member in (
            phase_of(x_wave, x_cells),
            phase_of(y_wave, row_count * y_cells),
            phase_of(z_wave, col_count * z_cells),
        )
    ]
    plus_symbols = [(jnp.cos(member) - 1.0, jnp.sin(member)) for member in angle_list]
    minus_symbols = [(1.0 - jnp.cos(member), jnp.sin(member)) for member in angle_list]
    spread = (
        4.0 * jnp.sin(0.5 * angle_list[0]) ** 2
        + 4.0 * jnp.sin(0.5 * angle_list[1]) ** 2
        + 4.0 * jnp.sin(0.5 * angle_list[2]) ** 2
    )
    zero_mode = (x_wave == 0) & (y_wave == 0) & (z_wave == 0)
    total_cells = float(x_cells * row_count * y_cells * col_count * z_cells)
    multiplier = jnp.where(
        zero_mode,
        0.0,
        1.0 / (REFERENCE_DIFFUSIVITY * jnp.where(zero_mode, 1.0, spread) * total_cells),
    )
    return (plus_symbols, minus_symbols, multiplier)


def times_symbol(symbol, pieces):
    symbol_real, symbol_imag = symbol
    return (
        symbol_real * pieces[0] - symbol_imag * pieces[1],
        symbol_real * pieces[1] + symbol_imag * pieces[0],
    )


def stack_symbols(symbols, pieces):
    products = [times_symbol(symbol, pieces) for symbol in symbols]
    return (
        jnp.concatenate([member[0] for member in products], axis=0),
        jnp.concatenate([member[1] for member in products], axis=0),
    )


def contract_symbols(symbols, pieces):
    real_sum = jnp.zeros_like(pieces[0][0:1])
    imag_sum = jnp.zeros_like(pieces[1][0:1])
    for direction in range(3):
        product = times_symbol(
            symbols[direction],
            (pieces[0][direction : direction + 1], pieces[1][direction : direction + 1]),
        )
        real_sum = real_sum + product[0]
        imag_sum = imag_sum + product[1]
    return (real_sum, imag_sum)


def rescale(multiplier, pieces):
    return (multiplier * pieces[0], multiplier * pieces[1])


def on_device_general(volume):
    z_cells, y_cells, x_cells = volume.shape
    smooth = volume
    for sweep_index in range(PASSES):
        padded = with_halo(smooth, (("row", 1), ("col", 0)), 1)
        smooth = diffuse(padded)
    diffusivity = LOW_DIFFUSIVITY + DIFFUSIVITY_SPAN * jax.nn.sigmoid(GRAY_SLOPE * smooth)
    excess = diffusivity - REFERENCE_DIFFUSIVITY
    plus_symbols, minus_symbols, multiplier = spectral_tables(z_cells, y_cells, x_cells)
    source = (excess - jnp.roll(excess, 1, axis=2))[None]
    potential_hat = rescale(multiplier, forward(source))
    unit_load = jnp.array([1.0, 0.0, 0.0], jnp.float32)[:, None, None, None]
    gradients = inverse(stack_symbols(plus_symbols, potential_hat), z_cells, y_cells, x_cells)
    tau_hat = forward(excess[None] * (gradients + unit_load))
    potential_hat = rescale(multiplier, contract_symbols(minus_symbols, tau_hat))
    gradient_x = inverse(times_symbol(plus_symbols[0], potential_hat), z_cells, y_cells, x_cells)[0]
    flux_x = diffusivity * (1.0 + gradient_x)
    return (smooth, flux_x)


MESH = pl.DeviceIdType.MESH
NT = (((1,), (1,)), ((), ()))
NN = (((1,), (0,)), ((), ()))
LANES = 128
SUBLANES = 8
EXCHANGES = PASSES + 1


def split(values):
    high = values.astype(jnp.bfloat16)
    return high, (values - high.astype(jnp.float32)).astype(jnp.bfloat16)


def split_numpy(values):
    high = values.astype(np.float32).astype(jnp.bfloat16)
    return high, (values - high.astype(np.float64)).astype(np.float32).astype(jnp.bfloat16)


def host_tables(rows, cols, z_cells, y_cells, x_cells):
    devices = rows * cols
    half = x_cells // 2
    k = np.arange(half)
    turn = 2.0 * np.pi * ((k[:, None] * np.arange(x_cells)[None, :]) % x_cells) / x_cells
    wave = np.stack([np.cos(turn), -np.sin(turn)])
    wave = wave.reshape(2, devices, SUBLANES, x_cells).transpose(1, 0, 2, 3)
    wave = wave.reshape(2 * half, x_cells)
    zl, yl = np.divmod(np.arange(LANES), y_cells)
    c, r = np.divmod(np.arange(devices), rows)
    inner = 2.0 * np.pi * (zl[:, None] * zl[None, :] / z_cells + yl[:, None] * yl[None, :] / y_cells)
    cosine, sine = np.cos(inner), np.sin(inner)
    plane = np.block([[cosine, -sine], [sine, cosine]])
    nz, ny = cols * z_cells, rows * y_cells
    twist = 2.0 * np.pi * (c[:, None] * zl[None, :] / nz + r[:, None] * yl[None, :] / ny)
    kz = c[:, None] + cols * zl[None, :]
    ky = r[:, None] + rows * yl[None, :]
    lam_zy = 4.0 * np.sin(np.pi * kz / nz) ** 2 + 4.0 * np.sin(np.pi * ky / ny) ** 2
    lam_x = (4.0 * np.sin(np.pi * k / x_cells) ** 2).reshape(devices, SUBLANES, 1)
    weight = np.where(k == 0, 1.0, 2.0) / (REFERENCE_DIFFUSIVITY * nz * ny * x_cells)
    weight = weight.reshape(devices, SUBLANES, 1)
    shape = (devices, SUBLANES, LANES)
    small = np.stack(
        [
            np.broadcast_to(np.cos(twist)[:, None, :], shape),
            np.broadcast_to(np.sin(twist)[:, None, :], shape),
            np.broadcast_to(lam_zy[:, None, :], shape),
            np.broadcast_to(lam_x, shape),
            np.broadcast_to(weight, shape),
        ]
    ).astype(np.float32)
    return split_numpy(wave) + split_numpy(plane) + (small,)


def small_fft(items, sign):
    size = len(items)
    if size == 1:
        return items
    even, odd = small_fft(items[::2], sign), small_fft(items[1::2], sign)
    low, high = [], []
    for k in range(size // 2):
        (er, ei), (xr, xi) = even[k], odd[k]
        if 4 * k == size:
            xr, xi = -sign * xi, sign * xr
        elif k:
            co, si = math.cos(2 * math.pi * k / size), sign * math.sin(2 * math.pi * k / size)
            xr, xi = xr * co - xi * si, xr * si + xi * co
        low.append((er + xr, ei + xi))
        high.append((er - xr, ei - xi))
    return low + high


def grid_fft(items, rows, cols, sign):
    lines = [small_fft(items[c * rows : (c + 1) * rows], sign) for c in range(cols)]
    columns = [small_fft([lines[c][r] for c in range(cols)], sign) for r in range(rows)]
    return [columns[r][c] for c in range(cols) for r in range(rows)]


def kernel(
    rows, cols, z_cells, y_cells, x_cells,
    volume, wave_hi_hbm, wave_lo_hbm, plane_hi_hbm, plane_lo_hbm, small_hbm,
    smooth_out, flux_out,
    wave_hi, wave_lo, plane_hi, plane_lo, small,
    field, excess_ref, y_send, y_recv, z_recv, ey_send, ey_recv, ez_recv,
    packed, arrived,
    table_sem, halo_send, halo_recv, e_send, e_recv, all_send, all_recv,
):
    devices = rows * cols
    cells = z_cells * y_cells
    row, col = lax.axis_index("row"), lax.axis_index("col")
    me = col * rows + row
    up_row, down_row = lax.rem(row + 1, rows), lax.rem(row + rows - 1, rows)
    up_col, down_col = lax.rem(col + 1, cols), lax.rem(col + cols - 1, cols)

    loads = [
        pltpu.make_async_copy(source, target, table_sem.at[i])
        for i, (source, target) in enumerate(
            (
                (wave_hi_hbm, wave_hi), (wave_lo_hbm, wave_lo), (plane_hi_hbm, plane_hi),
                (plane_lo_hbm, plane_lo), (small_hbm, small), (volume, field.at[0]),
            )
        )
    ]
    for load in loads:
        load.start()

    barrier = pltpu.get_barrier_semaphore()

    def greet(step, carry):
        other = lax.rem(me + step, devices)
        pl.semaphore_signal(
            barrier, inc=1, device_id=(lax.rem(other, rows), other // rows), device_id_type=MESH
        )
        return carry

    lax.fori_loop(1, devices, greet, 0)
    pl.semaphore_wait(barrier, devices - 1)

    place = lax.broadcasted_iota(jnp.int32, (cells, x_cells), 0)
    first_y = lax.rem(place, y_cells) == 0
    last_y = lax.rem(place, y_cells) == y_cells - 1

    def spread(edge):
        wide = jnp.broadcast_to(edge[:, None, :], (z_cells, y_cells, x_cells))
        return wide.reshape(cells, x_cells)

    def edge_of(values, y):
        return values.reshape(z_cells, y_cells, x_cells)[:, y, :]

    def remote(source, target, send, recv, device):
        return pltpu.make_async_remote_copy(
            src_ref=source, dst_ref=target, send_sem=send, recv_sem=recv,
            device_id=device, device_id_type=MESH,
        )

    def start_halo(e):
        y_send[e, 0] = edge_of(field[e], y_cells - 1)
        y_send[e, 1] = edge_of(field[e], 0)
        copies = (
            remote(y_send.at[e, 0], y_recv.at[e, 0], halo_send.at[e, 0], halo_recv.at[e, 0], (up_row, col)),
            remote(y_send.at[e, 1], y_recv.at[e, 1], halo_send.at[e, 1], halo_recv.at[e, 1], (down_row, col)),
            remote(field.at[e, pl.ds(cells - y_cells, y_cells)], z_recv.at[e, 0],
                   halo_send.at[e, 2], halo_recv.at[e, 2], (row, up_col)),
            remote(field.at[e, pl.ds(0, y_cells)], z_recv.at[e, 1],
                   halo_send.at[e, 3], halo_recv.at[e, 3], (row, down_col)),
        )
        for copy in copies:
            copy.start()
        return copies

    def next_x(v):
        return pltpu.roll(v, x_cells - 1, 1)

    def prev_x(v):
        return pltpu.roll(v, 1, 1)

    def limited(differ):
        scaled = differ / EDGE_SCALE
        return differ / (1.0 + scaled * scaled)

    pending = []
    loads.pop().wait()
    for sweep in range(PASSES):
        copies = start_halo(sweep)
        pending += copies
        now = field[sweep]
        flow = limited(next_x(now) - now)
        total = flow - prev_x(flow)
        inner_z = limited(now[y_cells:] - now[:-y_cells])
        for copy in copies:
            copy.wait_recv()
        above = jnp.where(last_y, spread(y_recv[sweep, 1]), pltpu.roll(now, cells - 1, 0))
        flow = limited(above - now)
        edge = limited(edge_of(now, 0) - y_recv[sweep, 0])
        total = total + (flow - jnp.where(first_y, spread(edge), pltpu.roll(flow, 1, 0)))
        z_low = limited(now[:y_cells] - z_recv[sweep, 0])
        z_high = limited(z_recv[sweep, 1] - now[-y_cells:])
        total = total + (
            jnp.concatenate([inner_z, z_high], axis=0) - jnp.concatenate([z_low, inner_z], axis=0)
        )
        later = now + TIME_STEP * total
        if sweep < PASSES - 1:
            field[sweep + 1] = later
    smooth_out[...] = later.reshape(z_cells, y_cells, x_cells)
    diffusivity = LOW_DIFFUSIVITY + DIFFUSIVITY_SPAN / (1.0 + jnp.exp(-GRAY_SLOPE * later))
    flux_out[...] = diffusivity.reshape(z_cells, y_cells, x_cells)
    excess = diffusivity - REFERENCE_DIFFUSIVITY
    excess_ref[...] = excess
    ey_send[...] = edge_of(excess, y_cells - 1)
    e_copies = (
        remote(ey_send, ey_recv, e_send.at[0], e_recv.at[0], (up_row, col)),
        remote(excess_ref.at[pl.ds(cells - y_cells, y_cells)], ez_recv, e_send.at[1], e_recv.at[1], (row, up_col)),
    )
    for copy in e_copies:
        copy.start()
    pending += e_copies
    for load in loads:
        load.wait()

    def exchange(turn):
        def send(step, carry):
            other = lax.rem(col + step, cols) * rows + lax.rem(row + step // cols, rows)
            remote(
                packed.at[turn, other], arrived.at[turn, me], all_send.at[turn], all_recv.at[turn],
                (lax.rem(other, rows), other // rows),
            ).start()
            return carry

        lax.fori_loop(1, devices, send, 0)
        arrived[turn, me] = packed[turn, me]
        block = arrived.at[turn, pl.ds(0, devices - 1)]
        pltpu.make_async_copy(block, block, all_recv.at[turn]).wait()

    def finish(turn):
        block = packed.at[turn, pl.ds(0, devices - 1)]
        pltpu.make_async_copy(block, block, all_send.at[turn]).wait()

    def product(a, b, dims):
        return lax.dot_general(a, b, dims, preferred_element_type=jnp.float32)

    def row_product(values, high, low, dims):
        values_hi, values_lo = split(values)
        count = values.shape[0]
        both = product(jnp.concatenate([values_hi, values_lo], axis=0), high, dims)
        return both[:count] + (both[count:] + product(values_hi, low, dims))

    def solve(source, turn):
        source_hi, source_lo = split(source)
        both = product(wave_hi[...], jnp.concatenate([source_hi, source_lo], axis=0), NT)
        spectrum = both[:, :cells] + (both[:, cells:] + product(wave_lo[...], source_hi, NT))
        packed[turn] = spectrum.reshape(devices, 2 * SUBLANES, LANES)
        exchange(turn)
        items = [(arrived[turn, d, :SUBLANES], arrived[turn, d, SUBLANES:]) for d in range(devices)]
        items = grid_fft(items, rows, cols, -1.0)
        turned = []
        for d, (re, im) in enumerate(items):
            co, si = small[0, d], small[1, d]
            turned.append(jnp.concatenate([re * co + im * si, im * co - re * si], axis=1))
        waves = row_product(jnp.concatenate(turned, axis=0), plane_hi[...], plane_lo[...], NN)
        lam = small[2] + small[3, me][None]
        factor = jnp.where(lam == 0.0, 0.0, small[4, me][None] / jnp.where(lam == 0.0, 1.0, lam))
        factor = factor.reshape(devices * SUBLANES, LANES)
        waves = waves * jnp.concatenate([factor, factor], axis=1)
        waves = row_product(waves, plane_hi[...], plane_lo[...], NT)
        items = []
        for d in range(devices):
            part = waves[d * SUBLANES : (d + 1) * SUBLANES]
            re, im = part[:, :LANES], part[:, LANES:]
            co, si = small[0, d], small[1, d]
            items.append((re * co - im * si, im * co + re * si))
        items = grid_fft(items, rows, cols, 1.0)
        for d, (re, im) in enumerate(items):
            packed[turn + 1, d, :SUBLANES] = re
            packed[turn + 1, d, SUBLANES:] = im
        exchange(turn + 1)
        back = arrived[turn + 1].reshape(2 * SUBLANES * devices, LANES)
        return row_product(back.T, wave_hi[...], wave_lo[...], NN)

    potential = solve(excess - prev_x(excess), 0)
    field[PASSES] = potential
    copies = start_halo(PASSES)
    pending += copies
    potential = field[PASSES]
    excess = excess_ref[...]
    tau = excess * (1.0 + (next_x(potential) - potential))
    diverge = tau - prev_x(tau)
    inner_z = excess[:-y_cells] * (potential[y_cells:] - potential[:-y_cells])
    for copy in e_copies + copies:
        copy.wait_recv()
    above = jnp.where(last_y, spread(y_recv[PASSES, 1]), pltpu.roll(potential, cells - 1, 0))
    tau = excess * (above - potential)
    edge = ey_recv[...] * (edge_of(potential, 0) - y_recv[PASSES, 0])
    diverge = diverge + (tau - jnp.where(first_y, spread(edge), pltpu.roll(tau, 1, 0)))
    z_low = ez_recv[...] * (potential[:y_cells] - z_recv[PASSES, 0])
    z_high = excess[-y_cells:] * (z_recv[PASSES, 1] - potential[-y_cells:])
    diverge = diverge + (
        jnp.concatenate([inner_z, z_high], axis=0) - jnp.concatenate([z_low, inner_z], axis=0)
    )
    potential = solve(diverge, 2)
    gradient = next_x(potential) - potential
    flux_out[...] = flux_out[...] * (1.0 + gradient.reshape(z_cells, y_cells, x_cells))
    for copy in pending:
        copy.wait_send()
    for turn in range(4):
        finish(turn)


def on_device(rows, cols, tables, volume):
    z_cells, y_cells, x_cells = volume.shape
    devices, cells = rows * cols, z_cells * y_cells
    f32, bf16 = jnp.float32, jnp.bfloat16
    vmem = pl.BlockSpec(memory_space=pltpu.VMEM)
    scratch = [pltpu.VMEM(table.shape, table.dtype) for table in tables] + [
        pltpu.VMEM((EXCHANGES, cells, x_cells), f32),
        pltpu.VMEM((cells, x_cells), f32),
        pltpu.VMEM((EXCHANGES, 2, z_cells, x_cells), f32),
        pltpu.VMEM((EXCHANGES, 2, z_cells, x_cells), f32),
        pltpu.VMEM((EXCHANGES, 2, y_cells, x_cells), f32),
        pltpu.VMEM((z_cells, x_cells), f32),
        pltpu.VMEM((z_cells, x_cells), f32),
        pltpu.VMEM((y_cells, x_cells), f32),
        pltpu.VMEM((4, devices, 2 * SUBLANES, LANES), f32),
        pltpu.VMEM((4, devices, 2 * SUBLANES, LANES), f32),
        pltpu.SemaphoreType.DMA((len(tables) + 1,)),
        pltpu.SemaphoreType.DMA((EXCHANGES, 4)),
        pltpu.SemaphoreType.DMA((EXCHANGES, 4)),
        pltpu.SemaphoreType.DMA((2,)),
        pltpu.SemaphoreType.DMA((2,)),
        pltpu.SemaphoreType.DMA((4,)),
        pltpu.SemaphoreType.DMA((4,)),
    ]
    shape = jax.ShapeDtypeStruct(volume.shape, f32)
    return pl.pallas_call(
        functools.partial(kernel, rows, cols, z_cells, y_cells, x_cells),
        out_shape=(shape, shape),
        in_specs=[pl.BlockSpec(memory_space=pl.ANY)] * (len(tables) + 1),
        out_specs=(vmem, vmem),
        scratch_shapes=scratch,
        compiler_params=pltpu.CompilerParams(
            collective_id=0, has_side_effects=True, vmem_limit_bytes=60 * 1024 * 1024
        ),
    )(volume.reshape(cells, x_cells), *tables)


def power_of_two(count):
    return count & (count - 1) == 0


def block_function(rows, cols, volume):
    z_cells, y_cells, x_cells = volume.shape
    devices = rows * cols
    direct = (
        x_cells // 2 == SUBLANES * devices
        and z_cells * y_cells == LANES
        and z_cells % 8 == 0
        and y_cells % 8 == 0
        and power_of_two(rows)
        and power_of_two(cols)
        and min(rows, cols) > 2
    )
    if not direct:
        return on_device_general(volume)
    tables = [jnp.asarray(t) for t in host_tables(rows, cols, z_cells, y_cells, x_cells)]
    return on_device(rows, cols, tables, volume)


def solution(mesh):
    return jax.shard_map(
        functools.partial(block_function, mesh.shape["row"], mesh.shape["col"]),
        mesh=mesh,
        in_specs=(P("col", "row", None),),
        out_specs=(P("col", "row", None), P("col", "row", None)),
        check_vma=False,
    )
```

```python
import functools
import math

import jax
import jax.numpy as jnp
import numpy as np
from jax import lax
from jax.experimental import pallas as pl
from jax.experimental.pallas import tpu as pltpu
from jax.sharding import PartitionSpec as P

PASSES = 3


HIGHEST = lax.Precision.HIGHEST
TIME_STEP = 0.16
EDGE_SCALE = 2.0
LOW_DIFFUSIVITY = 0.2
DIFFUSIVITY_SPAN = 1.8
GRAY_SLOPE = 2.5
REFERENCE_DIFFUSIVITY = 1.1


def with_halo(block, sides, width):
    for axis, dim in sides:
        count = lax.axis_size(axis)
        forward = [(i, i + 1) for i in range(count - 1)]
        forward.append((count - 1, 0))
        backward = [(target, source) for source, target in forward]
        low = lax.ppermute(
            lax.slice_in_dim(block, block.shape[dim] - width, None, axis=dim), axis, forward
        )
        high = lax.ppermute(lax.slice_in_dim(block, 0, width, axis=dim), axis, backward)
        block = jnp.concatenate([low, block, high], axis=dim)
    return block


def diffuse(padded):
    center = padded[1:-1, 1:-1, :]
    summed = jnp.zeros_like(center)
    neighbours = (
        padded[:-2, 1:-1, :],
        padded[2:, 1:-1, :],
        padded[1:-1, :-2, :],
        padded[1:-1, 2:, :],
        jnp.roll(center, 1, axis=2),
        jnp.roll(center, -1, axis=2),
    )
    for member in neighbours:
        differ = member - center
        summed = summed + differ / (1.0 + (differ / EDGE_SCALE) ** 2)
    return center + TIME_STEP * summed


def phase_of(integers, length):
    return (integers % length).astype(jnp.float32) * (2.0 * math.pi / length)


def dft_table(length):
    counter = jnp.arange(length, dtype=jnp.int32)
    angles = phase_of(counter[:, None] * counter[None, :], length)
    return (jnp.cos(angles), jnp.sin(angles))


def plane_table(z_cells, y_cells, along_z):
    counter = jnp.arange(z_cells * y_cells, dtype=jnp.int32)
    z_place = counter // y_cells
    y_place = counter % y_cells
    if along_z:
        same = y_place[:, None] == y_place[None, :]
        angles = phase_of(z_place[:, None] * z_place[None, :], z_cells)
    else:
        same = z_place[:, None] == z_place[None, :]
        angles = phase_of(y_place[:, None] * y_place[None, :], y_cells)
    return (jnp.where(same, jnp.cos(angles), 0.0), jnp.where(same, jnp.sin(angles), 0.0))


def contract(pieces, tables, pattern, orient):
    real_part, imag_part = pieces
    cosine, sine_part = tables
    real_cos = jnp.einsum(pattern, real_part, cosine, precision=HIGHEST)
    imag_sin = jnp.einsum(pattern, imag_part, sine_part, precision=HIGHEST)
    imag_cos = jnp.einsum(pattern, imag_part, cosine, precision=HIGHEST)
    real_sin = jnp.einsum(pattern, real_part, sine_part, precision=HIGHEST)
    return (real_cos - orient * imag_sin, imag_cos + orient * real_sin)


def rotate(pieces, angles, orient):
    cosine = jnp.cos(angles)
    sine_part = jnp.sin(angles)
    real_part, imag_part = pieces
    return (
        real_part * cosine - orient * imag_part * sine_part,
        imag_part * cosine + orient * real_part * sine_part,
    )


def y_twiddle(row_count, z_cells, y_cells):
    within = jnp.arange(z_cells * y_cells, dtype=jnp.int32) % y_cells
    orders = jnp.arange(row_count, dtype=jnp.int32)
    return phase_of(orders[:, None] * within[None, :], row_count * y_cells)[:, None, :]


def z_twiddle(col_count, z_cells, y_cells):
    within = jnp.arange(z_cells * y_cells, dtype=jnp.int32) // y_cells
    orders = jnp.arange(col_count, dtype=jnp.int32)
    return phase_of(orders[:, None] * within[None, :], col_count * z_cells)[:, None, None, :]


def row_transpose(pieces):
    return (
        lax.all_to_all(pieces[0], "row", split_axis=1, concat_axis=1, tiled=True),
        lax.all_to_all(pieces[1], "row", split_axis=1, concat_axis=1, tiled=True),
    )


def col_transpose(pieces):
    return (
        lax.all_to_all(pieces[0], "col", split_axis=1, concat_axis=1, tiled=True),
        lax.all_to_all(pieces[1], "col", split_axis=1, concat_axis=1, tiled=True),
    )


def reshape_all(pieces, extent):
    return (pieces[0].reshape(extent), pieces[1].reshape(extent))


def forward(source):
    fields, z_cells, y_cells, x_cells = source.shape
    row_count = lax.axis_size("row")
    col_count = lax.axis_size("col")
    half_width = x_cells // 2
    per_row = half_width // row_count
    block_share = row_count // col_count
    plane_cells = z_cells * y_cells
    flat = source.reshape(fields, plane_cells, x_cells)
    x_index = jnp.arange(x_cells, dtype=jnp.int32)
    k_index = jnp.arange(half_width, dtype=jnp.int32)
    angles = phase_of(x_index[:, None] * k_index[None, :], x_cells)
    real_part = jnp.einsum("fmx,xk->fkm", flat, jnp.cos(angles), precision=HIGHEST)
    imag_part = -jnp.einsum("fmx,xk->fkm", flat, jnp.sin(angles), precision=HIGHEST)
    pieces = reshape_all((real_part, imag_part), (fields, row_count, per_row, plane_cells))
    pieces = row_transpose(pieces)
    pieces = contract(pieces, dft_table(row_count), "fskm,sp->fpkm", -1.0)
    pieces = rotate(pieces, y_twiddle(row_count, z_cells, y_cells), -1.0)
    pieces = contract(pieces, plane_table(z_cells, y_cells, False), "fpkm,mn->fpkn", -1.0)
    pieces = reshape_all(pieces, (fields, col_count, block_share * per_row * plane_cells))
    pieces = col_transpose(pieces)
    pieces = reshape_all(pieces, (fields, col_count, block_share, per_row, plane_cells))
    pieces = contract(pieces, dft_table(col_count), "fcabm,cp->fpabm", -1.0)
    pieces = rotate(pieces, z_twiddle(col_count, z_cells, y_cells), -1.0)
    return contract(pieces, plane_table(z_cells, y_cells, True), "fpabm,mn->fpabn", -1.0)


def inverse(pieces, z_cells, y_cells, x_cells):
    fields, col_count, block_share, per_row, plane_cells = pieces[0].shape
    row_count = col_count * block_share
    half_width = row_count * per_row
    pieces = contract(pieces, plane_table(z_cells, y_cells, True), "fpabn,nm->fpabm", 1.0)
    pieces = rotate(pieces, z_twiddle(col_count, z_cells, y_cells), 1.0)
    pieces = contract(pieces, dft_table(col_count), "fpabm,pc->fcabm", 1.0)
    pieces = reshape_all(pieces, (fields, col_count, block_share * per_row * plane_cells))
    pieces = col_transpose(pieces)
    pieces = reshape_all(pieces, (fields, row_count, per_row, plane_cells))
    pieces = contract(pieces, plane_table(z_cells, y_cells, False), "fpkn,nm->fpkm", 1.0)
    pieces = rotate(pieces, y_twiddle(row_count, z_cells, y_cells), 1.0)
    pieces = contract(pieces, dft_table(row_count), "fpkm,ps->fskm", 1.0)
    pieces = row_transpose(pieces)
    pieces = reshape_all(pieces, (fields, half_width, plane_cells))
    k_index = jnp.arange(half_width, dtype=jnp.int32)
    x_index = jnp.arange(x_cells, dtype=jnp.int32)
    angles = phase_of(k_index[:, None] * x_index[None, :], x_cells)
    weight = jnp.where(k_index == 0, 1.0, 2.0).astype(jnp.float32)[:, None]
    real_out = jnp.einsum("fkm,kx->fmx", pieces[0], weight * jnp.cos(angles), precision=HIGHEST)
    imag_out = jnp.einsum("fkm,kx->fmx", pieces[1], weight * jnp.sin(angles), precision=HIGHEST)
    return (real_out - imag_out).reshape(fields, z_cells, y_cells, x_cells)


def spectral_tables(z_cells, y_cells, x_cells):
    row_count = lax.axis_size("row")
    col_count = lax.axis_size("col")
    block_share = row_count // col_count
    per_row = x_cells // 2 // row_count
    plane = jnp.arange(z_cells * y_cells, dtype=jnp.int32)
    z_wave = (
        jnp.arange(col_count, dtype=jnp.int32)[:, None, None, None]
        + col_count * (plane // y_cells)[None, None, None, :]
    )
    y_wave = (lax.axis_index("col") * block_share + jnp.arange(block_share, dtype=jnp.int32))[
        None, :, None, None
    ] + row_count * (plane % y_cells)[None, None, None, :]
    x_wave = (lax.axis_index("row") * per_row + jnp.arange(per_row, dtype=jnp.int32))[
        None, None, :, None
    ]
    k_extent = (col_count, block_share, per_row, z_cells * y_cells)
    angle_list = [
        jnp.broadcast_to(member, k_extent)
        for member in (
            phase_of(x_wave, x_cells),
            phase_of(y_wave, row_count * y_cells),
            phase_of(z_wave, col_count * z_cells),
        )
    ]
    plus_symbols = [(jnp.cos(member) - 1.0, jnp.sin(member)) for member in angle_list]
    minus_symbols = [(1.0 - jnp.cos(member), jnp.sin(member)) for member in angle_list]
    spread = (
        4.0 * jnp.sin(0.5 * angle_list[0]) ** 2
        + 4.0 * jnp.sin(0.5 * angle_list[1]) ** 2
        + 4.0 * jnp.sin(0.5 * angle_list[2]) ** 2
    )
    zero_mode = (x_wave == 0) & (y_wave == 0) & (z_wave == 0)
    total_cells = float(x_cells * row_count * y_cells * col_count * z_cells)
    multiplier = jnp.where(
        zero_mode,
        0.0,
        1.0 / (REFERENCE_DIFFUSIVITY * jnp.where(zero_mode, 1.0, spread) * total_cells),
    )
    return (plus_symbols, minus_symbols, multiplier)


def times_symbol(symbol, pieces):
    symbol_real, symbol_imag = symbol
    return (
        symbol_real * pieces[0] - symbol_imag * pieces[1],
        symbol_real * pieces[1] + symbol_imag * pieces[0],
    )


def stack_symbols(symbols, pieces):
    products = [times_symbol(symbol, pieces) for symbol in symbols]
    return (
        jnp.concatenate([member[0] for member in products], axis=0),
        jnp.concatenate([member[1] for member in products], axis=0),
    )


def contract_symbols(symbols, pieces):
    real_sum = jnp.zeros_like(pieces[0][0:1])
    imag_sum = jnp.zeros_like(pieces[1][0:1])
    for direction in range(3):
        product = times_symbol(
            symbols[direction],
            (pieces[0][direction : direction + 1], pieces[1][direction : direction + 1]),
        )
        real_sum = real_sum + product[0]
        imag_sum = imag_sum + product[1]
    return (real_sum, imag_sum)


def rescale(multiplier, pieces):
    return (multiplier * pieces[0], multiplier * pieces[1])


def on_device_general(volume):
    z_cells, y_cells, x_cells = volume.shape
    smooth = volume
    for sweep_index in range(PASSES):
        padded = with_halo(smooth, (("row", 1), ("col", 0)), 1)
        smooth = diffuse(padded)
    diffusivity = LOW_DIFFUSIVITY + DIFFUSIVITY_SPAN * jax.nn.sigmoid(GRAY_SLOPE * smooth)
    excess = diffusivity - REFERENCE_DIFFUSIVITY
    plus_symbols, minus_symbols, multiplier = spectral_tables(z_cells, y_cells, x_cells)
    source = (excess - jnp.roll(excess, 1, axis=2))[None]
    potential_hat = rescale(multiplier, forward(source))
    unit_load = jnp.array([1.0, 0.0, 0.0], jnp.float32)[:, None, None, None]
    gradients = inverse(stack_symbols(plus_symbols, potential_hat), z_cells, y_cells, x_cells)
    tau_hat = forward(excess[None] * (gradients + unit_load))
    potential_hat = rescale(multiplier, contract_symbols(minus_symbols, tau_hat))
    gradient_x = inverse(times_symbol(plus_symbols[0], potential_hat), z_cells, y_cells, x_cells)[0]
    flux_x = diffusivity * (1.0 + gradient_x)
    return (smooth, flux_x)


MESH = pl.DeviceIdType.MESH
NT = (((1,), (1,)), ((), ()))
NN = (((1,), (0,)), ((), ()))
LANES = 128
SUBLANES = 8
HALVES = 2
QUADS = 4
EXCHANGES = PASSES + 1


def split(values):
    high = values.astype(jnp.bfloat16)
    return high, (values - high.astype(jnp.float32)).astype(jnp.bfloat16)


def split_numpy(values):
    high = values.astype(np.float32).astype(jnp.bfloat16)
    return high, (values - high.astype(np.float64)).astype(np.float32).astype(jnp.bfloat16)


def host_tables(rows, cols, z_cells, y_cells, x_cells):
    devices = rows * cols
    waves = x_cells // 2
    k = np.arange(waves)
    turn = 2.0 * np.pi * ((k[:, None] * np.arange(x_cells)[None, :]) % x_cells) / x_cells
    wave = np.stack([np.cos(turn), -np.sin(turn)])
    wave = wave.reshape(2, devices, HALVES, QUADS, x_cells).transpose(2, 1, 0, 3, 4)
    wave = wave.reshape(2 * waves, x_cells)
    zl, yl = np.divmod(np.arange(LANES), y_cells)
    c, r = np.divmod(np.arange(devices), rows)
    inner = 2.0 * np.pi * (zl[:, None] * zl[None, :] / z_cells + yl[:, None] * yl[None, :] / y_cells)
    cosine, sine = np.cos(inner), np.sin(inner)
    plane = np.concatenate([cosine, sine], axis=1)
    nz, ny = cols * z_cells, rows * y_cells
    twist = 2.0 * np.pi * (c[:, None] * zl[None, :] / nz + r[:, None] * yl[None, :] / ny)
    kz = c[:, None] + cols * zl[None, :]
    ky = r[:, None] + rows * yl[None, :]
    lam_zy = 4.0 * np.sin(np.pi * kz / nz) ** 2 + 4.0 * np.sin(np.pi * ky / ny) ** 2
    lam_x = 4.0 * np.sin(np.pi * k / x_cells) ** 2
    weight = np.where(k == 0, 1.0, 2.0) / (REFERENCE_DIFFUSIVITY * nz * ny * x_cells)
    shape = (devices, SUBLANES, LANES)
    sign = np.where(np.arange(SUBLANES) < QUADS, 1.0, -1.0)[None, :, None]
    members = [np.cos(twist)[:, None, :], np.sin(twist)[:, None, :] * sign, lam_zy[:, None, :]]
    for member in (lam_x, weight):
        member = member.reshape(devices, HALVES, 1, QUADS)
        member = np.broadcast_to(member, (devices, HALVES, 2, QUADS))
        for half in range(HALVES):
            members.append(member[:, half].reshape(devices, SUBLANES, 1))
    small = np.stack([np.broadcast_to(m, shape) for m in members]).astype(np.float32)
    return split_numpy(wave) + split_numpy(plane) + (small,)


def small_fft(items, sign, turned):
    size = len(items)
    if size == 1:
        return items
    even, odd = small_fft(items[::2], sign, turned), small_fft(items[1::2], sign, turned)
    low, high = [], []
    for k in range(size // 2):
        item = odd[k]
        if 4 * k == size:
            item = -sign * turned(item)
        elif k:
            angle = 2 * math.pi * k / size
            item = math.cos(angle) * item - (sign * math.sin(angle)) * turned(item)
        low.append(even[k] + item)
        high.append(even[k] - item)
    return low + high


def grid_fft(items, rows, cols, sign, turned):
    lines = [small_fft(items[c * rows : (c + 1) * rows], sign, turned) for c in range(cols)]
    columns = [small_fft([lines[c][r] for c in range(cols)], sign, turned) for r in range(rows)]
    return [columns[r][c] for c in range(cols) for r in range(rows)]


def kernel(
    rows, cols, z_cells, y_cells, x_cells,
    volume, wave_hi_hbm, wave_lo_hbm, plane_hi_hbm, plane_lo_hbm, small_hbm,
    smooth_out, flux_out,
    wave_hi, wave_lo, plane_hi, plane_lo, small,
    field, excess_ref, y_send, y_recv, z_recv, ey_send, ey_recv, ez_recv,
    packed, arrived,
    table_sem, halo_send, halo_recv, e_send, e_recv, all_send, all_recv,
):
    devices = rows * cols
    cells = z_cells * y_cells
    row, col = lax.axis_index("row"), lax.axis_index("col")
    me = col * rows + row
    up_row, down_row = lax.rem(row + 1, rows), lax.rem(row + rows - 1, rows)
    up_col, down_col = lax.rem(col + 1, cols), lax.rem(col + cols - 1, cols)

    loads = [
        pltpu.make_async_copy(source, target, table_sem.at[i])
        for i, (source, target) in enumerate(
            (
                (wave_hi_hbm, wave_hi), (wave_lo_hbm, wave_lo), (plane_hi_hbm, plane_hi),
                (plane_lo_hbm, plane_lo), (small_hbm, small), (volume, field.at[0]),
            )
        )
    ]
    for load in loads:
        load.start()

    barrier = pltpu.get_barrier_semaphore()

    def greet(step, carry):
        other = lax.rem(me + step, devices)
        pl.semaphore_signal(
            barrier, inc=1, device_id=(lax.rem(other, rows), other // rows), device_id_type=MESH
        )
        return carry

    lax.fori_loop(1, devices, greet, 0)
    pl.semaphore_wait(barrier, devices - 1)

    place = lax.broadcasted_iota(jnp.int32, (cells, x_cells), 0)
    first_y = lax.rem(place, y_cells) == 0
    last_y = lax.rem(place, y_cells) == y_cells - 1

    def spread(edge):
        wide = jnp.broadcast_to(edge[:, None, :], (z_cells, y_cells, x_cells))
        return wide.reshape(cells, x_cells)

    def edge_of(values, y):
        return values.reshape(z_cells, y_cells, x_cells)[:, y, :]

    def remote(source, target, send, recv, device):
        return pltpu.make_async_remote_copy(
            src_ref=source, dst_ref=target, send_sem=send, recv_sem=recv,
            device_id=device, device_id_type=MESH,
        )

    def start_halo(e):
        y_send[e, 0] = edge_of(field[e], y_cells - 1)
        y_send[e, 1] = edge_of(field[e], 0)
        copies = (
            remote(y_send.at[e, 0], y_recv.at[e, 0], halo_send.at[e, 0], halo_recv.at[e, 0], (up_row, col)),
            remote(y_send.at[e, 1], y_recv.at[e, 1], halo_send.at[e, 1], halo_recv.at[e, 1], (down_row, col)),
            remote(field.at[e, pl.ds(cells - y_cells, y_cells)], z_recv.at[e, 0],
                   halo_send.at[e, 2], halo_recv.at[e, 2], (row, up_col)),
            remote(field.at[e, pl.ds(0, y_cells)], z_recv.at[e, 1],
                   halo_send.at[e, 3], halo_recv.at[e, 3], (row, down_col)),
        )
        for copy in copies:
            copy.start()
        return copies

    def next_x(v):
        return pltpu.roll(v, x_cells - 1, 1)

    def prev_x(v):
        return pltpu.roll(v, 1, 1)

    def limited(differ):
        scaled = differ / EDGE_SCALE
        return differ / (1.0 + scaled * scaled)

    pending = []
    loads.pop().wait()
    for sweep in range(PASSES):
        copies = start_halo(sweep)
        pending += copies
        now = field[sweep]
        flow = limited(next_x(now) - now)
        total = flow - prev_x(flow)
        inner_z = limited(now[y_cells:] - now[:-y_cells])
        for copy in copies:
            copy.wait_recv()
        above = jnp.where(last_y, spread(y_recv[sweep, 1]), pltpu.roll(now, cells - 1, 0))
        flow = limited(above - now)
        edge = limited(edge_of(now, 0) - y_recv[sweep, 0])
        total = total + (flow - jnp.where(first_y, spread(edge), pltpu.roll(flow, 1, 0)))
        z_low = limited(now[:y_cells] - z_recv[sweep, 0])
        z_high = limited(z_recv[sweep, 1] - now[-y_cells:])
        total = total + (
            jnp.concatenate([inner_z, z_high], axis=0) - jnp.concatenate([z_low, inner_z], axis=0)
        )
        later = now + TIME_STEP * total
        if sweep < PASSES - 1:
            field[sweep + 1] = later
    smooth_out[...] = later.reshape(z_cells, y_cells, x_cells)
    diffusivity = LOW_DIFFUSIVITY + DIFFUSIVITY_SPAN / (1.0 + jnp.exp(-GRAY_SLOPE * later))
    flux_out[...] = diffusivity.reshape(z_cells, y_cells, x_cells)
    excess = diffusivity - REFERENCE_DIFFUSIVITY
    excess_ref[...] = excess
    ey_send[...] = edge_of(excess, y_cells - 1)
    e_copies = (
        remote(ey_send, ey_recv, e_send.at[0], e_recv.at[0], (up_row, col)),
        remote(excess_ref.at[pl.ds(cells - y_cells, y_cells)], ez_recv, e_send.at[1], e_recv.at[1], (row, up_col)),
    )
    for copy in e_copies:
        copy.start()
    pending += e_copies
    for load in loads:
        load.wait()

    def start_exchange(turn, half):
        def send(step, carry):
            to_row = lax.rem(row + step // cols, rows)
            to_col = lax.rem(col + step, cols)
            remote(
                packed.at[turn, half, to_col * rows + to_row], arrived.at[turn, half, me],
                all_send.at[turn, half], all_recv.at[turn, half], (to_row, to_col),
            ).start()
            return carry

        lax.fori_loop(1, devices, send, 0)
        arrived[turn, half, me] = packed[turn, half, me]

    def end_exchange(turn, half):
        block = arrived.at[turn, half, pl.ds(0, devices - 1)]
        pltpu.make_async_copy(block, block, all_recv.at[turn, half]).wait()

    def finish(turn, half):
        block = packed.at[turn, half, pl.ds(0, devices - 1)]
        pltpu.make_async_copy(block, block, all_send.at[turn, half]).wait()

    real_rows = lax.broadcasted_iota(jnp.int32, (SUBLANES, LANES), 0) < QUADS

    def swapped(tile):
        return pltpu.roll(tile, QUADS, 0)

    def turned(tile):
        tile = swapped(tile)
        return jnp.where(real_rows, tile, -tile)

    def product(a, b, dims):
        return lax.dot_general(a, b, dims, preferred_element_type=jnp.float32)

    def row_product(values, high, low, dims):
        values_hi, values_lo = split(values)
        count = values.shape[0]
        both = product(jnp.concatenate([values_hi, values_lo], axis=0), high, dims)
        return both[:count] + (both[count:] + product(values_hi, low, dims))

    many = devices * SUBLANES
    side = lax.rem(lax.broadcasted_iota(jnp.int32, (many, LANES), 0), SUBLANES) < QUADS

    def plane_product(values, sign):
        both = row_product(values, plane_hi[...], plane_lo[...], NN)
        cosine, sine = both[:, :LANES], both[:, LANES:]
        sine = jnp.where(side, pltpu.roll(sine, many - QUADS, 0), -pltpu.roll(sine, QUADS, 0))
        return cosine - sign * sine

    def spectral(turn, half):
        items = [arrived[turn, half, d] for d in range(devices)]
        items = grid_fft(items, rows, cols, -1.0, turned)
        items = [t * small[0, d] + swapped(t) * small[1, d] for d, t in enumerate(items)]
        waves = plane_product(jnp.concatenate(items, axis=0), -1.0)
        lam = small[2] + small[3 + half, me][None]
        weight = small[3 + HALVES + half, me][None]
        factor = jnp.where(lam == 0.0, 0.0, weight / jnp.where(lam == 0.0, 1.0, lam))
        waves = plane_product(waves * factor.reshape(many, LANES), 1.0)
        items = [waves[d * SUBLANES : (d + 1) * SUBLANES] for d in range(devices)]
        items = [t * small[0, d] - swapped(t) * small[1, d] for d, t in enumerate(items)]
        for d, t in enumerate(grid_fft(items, rows, cols, 1.0, turned)):
            packed[turn + 1, half, d] = t

    def solve(source, turn):
        source_hi, source_lo = split(source)
        sources = jnp.concatenate([source_hi, source_lo], axis=0)
        for half in range(HALVES):
            part = pl.ds(half * many, many)
            both = product(wave_hi[part, :], sources, NT)
            spectrum = both[:, :cells] + (
                both[:, cells:] + product(wave_lo[part, :], source_hi, NT)
            )
            packed[turn, half] = spectrum.reshape(devices, SUBLANES, LANES)
            start_exchange(turn, half)
        for half in range(HALVES):
            end_exchange(turn, half)
            spectral(turn, half)
            start_exchange(turn + 1, half)
        total = None
        for half in range(HALVES):
            part = pl.ds(half * many, many)
            end_exchange(turn + 1, half)
            back = arrived[turn + 1, half].reshape(many, LANES)
            piece = row_product(back.T, wave_hi[part, :], wave_lo[part, :], NN)
            total = piece if half == 0 else total + piece
        return total

    potential = solve(excess - prev_x(excess), 0)
    field[PASSES] = potential
    copies = start_halo(PASSES)
    pending += copies
    potential = field[PASSES]
    excess = excess_ref[...]
    tau = excess * (1.0 + (next_x(potential) - potential))
    diverge = tau - prev_x(tau)
    inner_z = excess[:-y_cells] * (potential[y_cells:] - potential[:-y_cells])
    for copy in e_copies + copies:
        copy.wait_recv()
    above = jnp.where(last_y, spread(y_recv[PASSES, 1]), pltpu.roll(potential, cells - 1, 0))
    tau = excess * (above - potential)
    edge = ey_recv[...] * (edge_of(potential, 0) - y_recv[PASSES, 0])
    diverge = diverge + (tau - jnp.where(first_y, spread(edge), pltpu.roll(tau, 1, 0)))
    z_low = ez_recv[...] * (potential[:y_cells] - z_recv[PASSES, 0])
    z_high = excess[-y_cells:] * (z_recv[PASSES, 1] - potential[-y_cells:])
    diverge = diverge + (
        jnp.concatenate([inner_z, z_high], axis=0) - jnp.concatenate([z_low, inner_z], axis=0)
    )
    potential = solve(diverge, 2)
    gradient = next_x(potential) - potential
    flux_out[...] = flux_out[...] * (1.0 + gradient.reshape(z_cells, y_cells, x_cells))
    for copy in pending:
        copy.wait_send()
    for turn in range(4):
        for half in range(HALVES):
            finish(turn, half)


def on_device(rows, cols, tables, volume):
    z_cells, y_cells, x_cells = volume.shape
    devices, cells = rows * cols, z_cells * y_cells
    f32, bf16 = jnp.float32, jnp.bfloat16
    vmem = pl.BlockSpec(memory_space=pltpu.VMEM)
    scratch = [pltpu.VMEM(table.shape, table.dtype) for table in tables] + [
        pltpu.VMEM((EXCHANGES, cells, x_cells), f32),
        pltpu.VMEM((cells, x_cells), f32),
        pltpu.VMEM((EXCHANGES, 2, z_cells, x_cells), f32),
        pltpu.VMEM((EXCHANGES, 2, z_cells, x_cells), f32),
        pltpu.VMEM((EXCHANGES, 2, y_cells, x_cells), f32),
        pltpu.VMEM((z_cells, x_cells), f32),
        pltpu.VMEM((z_cells, x_cells), f32),
        pltpu.VMEM((y_cells, x_cells), f32),
        pltpu.VMEM((4, HALVES, devices, SUBLANES, LANES), f32),
        pltpu.VMEM((4, HALVES, devices, SUBLANES, LANES), f32),
        pltpu.SemaphoreType.DMA((len(tables) + 1,)),
        pltpu.SemaphoreType.DMA((EXCHANGES, 4)),
        pltpu.SemaphoreType.DMA((EXCHANGES, 4)),
        pltpu.SemaphoreType.DMA((2,)),
        pltpu.SemaphoreType.DMA((2,)),
        pltpu.SemaphoreType.DMA((4, HALVES)),
        pltpu.SemaphoreType.DMA((4, HALVES)),
    ]
    shape = jax.ShapeDtypeStruct(volume.shape, f32)
    return pl.pallas_call(
        functools.partial(kernel, rows, cols, z_cells, y_cells, x_cells),
        out_shape=(shape, shape),
        in_specs=[pl.BlockSpec(memory_space=pl.ANY)] * (len(tables) + 1),
        out_specs=(vmem, vmem),
        scratch_shapes=scratch,
        compiler_params=pltpu.CompilerParams(
            collective_id=0, has_side_effects=True, vmem_limit_bytes=60 * 1024 * 1024
        ),
    )(volume.reshape(cells, x_cells), *tables)


def power_of_two(count):
    return count & (count - 1) == 0


def block_function(rows, cols, volume):
    z_cells, y_cells, x_cells = volume.shape
    devices = rows * cols
    direct = (
        x_cells // 2 == SUBLANES * devices
        and z_cells * y_cells == LANES
        and z_cells % 8 == 0
        and y_cells % 8 == 0
        and power_of_two(rows)
        and power_of_two(cols)
        and min(rows, cols) > 2
    )
    if not direct:
        return on_device_general(volume)
    tables = [jnp.asarray(t) for t in host_tables(rows, cols, z_cells, y_cells, x_cells)]
    return on_device(rows, cols, tables, volume)


def solution(mesh):
    return jax.shard_map(
        functools.partial(block_function, mesh.shape["row"], mesh.shape["col"]),
        mesh=mesh,
        in_specs=(P("col", "row", None),),
        out_specs=(P("col", "row", None), P("col", "row", None)),
        check_vma=False,
    )
```

```python
import functools
import math

import jax
import jax.numpy as jnp
import numpy as np
from jax import lax
from jax.experimental import pallas as pl
from jax.experimental.pallas import tpu as pltpu
from jax.sharding import PartitionSpec as P

PASSES = 3


HIGHEST = lax.Precision.HIGHEST
TIME_STEP = 0.16
EDGE_SCALE = 2.0
LOW_DIFFUSIVITY = 0.2
DIFFUSIVITY_SPAN = 1.8
GRAY_SLOPE = 2.5
REFERENCE_DIFFUSIVITY = 1.1


def with_halo(block, sides, width):
    for axis, dim in sides:
        count = lax.axis_size(axis)
        forward = [(i, i + 1) for i in range(count - 1)]
        forward.append((count - 1, 0))
        backward = [(target, source) for source, target in forward]
        low = lax.ppermute(
            lax.slice_in_dim(block, block.shape[dim] - width, None, axis=dim), axis, forward
        )
        high = lax.ppermute(lax.slice_in_dim(block, 0, width, axis=dim), axis, backward)
        block = jnp.concatenate([low, block, high], axis=dim)
    return block


def diffuse(padded):
    center = padded[1:-1, 1:-1, :]
    summed = jnp.zeros_like(center)
    neighbours = (
        padded[:-2, 1:-1, :],
        padded[2:, 1:-1, :],
        padded[1:-1, :-2, :],
        padded[1:-1, 2:, :],
        jnp.roll(center, 1, axis=2),
        jnp.roll(center, -1, axis=2),
    )
    for member in neighbours:
        differ = member - center
        summed = summed + differ / (1.0 + (differ / EDGE_SCALE) ** 2)
    return center + TIME_STEP * summed


def phase_of(integers, length):
    return (integers % length).astype(jnp.float32) * (2.0 * math.pi / length)


def dft_table(length):
    counter = jnp.arange(length, dtype=jnp.int32)
    angles = phase_of(counter[:, None] * counter[None, :], length)
    return (jnp.cos(angles), jnp.sin(angles))


def plane_table(z_cells, y_cells, along_z):
    counter = jnp.arange(z_cells * y_cells, dtype=jnp.int32)
    z_place = counter // y_cells
    y_place = counter % y_cells
    if along_z:
        same = y_place[:, None] == y_place[None, :]
        angles = phase_of(z_place[:, None] * z_place[None, :], z_cells)
    else:
        same = z_place[:, None] == z_place[None, :]
        angles = phase_of(y_place[:, None] * y_place[None, :], y_cells)
    return (jnp.where(same, jnp.cos(angles), 0.0), jnp.where(same, jnp.sin(angles), 0.0))


def contract(pieces, tables, pattern, orient):
    real_part, imag_part = pieces
    cosine, sine_part = tables
    real_cos = jnp.einsum(pattern, real_part, cosine, precision=HIGHEST)
    imag_sin = jnp.einsum(pattern, imag_part, sine_part, precision=HIGHEST)
    imag_cos = jnp.einsum(pattern, imag_part, cosine, precision=HIGHEST)
    real_sin = jnp.einsum(pattern, real_part, sine_part, precision=HIGHEST)
    return (real_cos - orient * imag_sin, imag_cos + orient * real_sin)


def rotate(pieces, angles, orient):
    cosine = jnp.cos(angles)
    sine_part = jnp.sin(angles)
    real_part, imag_part = pieces
    return (
        real_part * cosine - orient * imag_part * sine_part,
        imag_part * cosine + orient * real_part * sine_part,
    )


def y_twiddle(row_count, z_cells, y_cells):
    within = jnp.arange(z_cells * y_cells, dtype=jnp.int32) % y_cells
    orders = jnp.arange(row_count, dtype=jnp.int32)
    return phase_of(orders[:, None] * within[None, :], row_count * y_cells)[:, None, :]


def z_twiddle(col_count, z_cells, y_cells):
    within = jnp.arange(z_cells * y_cells, dtype=jnp.int32) // y_cells
    orders = jnp.arange(col_count, dtype=jnp.int32)
    return phase_of(orders[:, None] * within[None, :], col_count * z_cells)[:, None, None, :]


def row_transpose(pieces):
    return (
        lax.all_to_all(pieces[0], "row", split_axis=1, concat_axis=1, tiled=True),
        lax.all_to_all(pieces[1], "row", split_axis=1, concat_axis=1, tiled=True),
    )


def col_transpose(pieces):
    return (
        lax.all_to_all(pieces[0], "col", split_axis=1, concat_axis=1, tiled=True),
        lax.all_to_all(pieces[1], "col", split_axis=1, concat_axis=1, tiled=True),
    )


def reshape_all(pieces, extent):
    return (pieces[0].reshape(extent), pieces[1].reshape(extent))


def forward(source):
    fields, z_cells, y_cells, x_cells = source.shape
    row_count = lax.axis_size("row")
    col_count = lax.axis_size("col")
    half_width = x_cells // 2
    per_row = half_width // row_count
    block_share = row_count // col_count
    plane_cells = z_cells * y_cells
    flat = source.reshape(fields, plane_cells, x_cells)
    x_index = jnp.arange(x_cells, dtype=jnp.int32)
    k_index = jnp.arange(half_width, dtype=jnp.int32)
    angles = phase_of(x_index[:, None] * k_index[None, :], x_cells)
    real_part = jnp.einsum("fmx,xk->fkm", flat, jnp.cos(angles), precision=HIGHEST)
    imag_part = -jnp.einsum("fmx,xk->fkm", flat, jnp.sin(angles), precision=HIGHEST)
    pieces = reshape_all((real_part, imag_part), (fields, row_count, per_row, plane_cells))
    pieces = row_transpose(pieces)
    pieces = contract(pieces, dft_table(row_count), "fskm,sp->fpkm", -1.0)
    pieces = rotate(pieces, y_twiddle(row_count, z_cells, y_cells), -1.0)
    pieces = contract(pieces, plane_table(z_cells, y_cells, False), "fpkm,mn->fpkn", -1.0)
    pieces = reshape_all(pieces, (fields, col_count, block_share * per_row * plane_cells))
    pieces = col_transpose(pieces)
    pieces = reshape_all(pieces, (fields, col_count, block_share, per_row, plane_cells))
    pieces = contract(pieces, dft_table(col_count), "fcabm,cp->fpabm", -1.0)
    pieces = rotate(pieces, z_twiddle(col_count, z_cells, y_cells), -1.0)
    return contract(pieces, plane_table(z_cells, y_cells, True), "fpabm,mn->fpabn", -1.0)


def inverse(pieces, z_cells, y_cells, x_cells):
    fields, col_count, block_share, per_row, plane_cells = pieces[0].shape
    row_count = col_count * block_share
    half_width = row_count * per_row
    pieces = contract(pieces, plane_table(z_cells, y_cells, True), "fpabn,nm->fpabm", 1.0)
    pieces = rotate(pieces, z_twiddle(col_count, z_cells, y_cells), 1.0)
    pieces = contract(pieces, dft_table(col_count), "fpabm,pc->fcabm", 1.0)
    pieces = reshape_all(pieces, (fields, col_count, block_share * per_row * plane_cells))
    pieces = col_transpose(pieces)
    pieces = reshape_all(pieces, (fields, row_count, per_row, plane_cells))
    pieces = contract(pieces, plane_table(z_cells, y_cells, False), "fpkn,nm->fpkm", 1.0)
    pieces = rotate(pieces, y_twiddle(row_count, z_cells, y_cells), 1.0)
    pieces = contract(pieces, dft_table(row_count), "fpkm,ps->fskm", 1.0)
    pieces = row_transpose(pieces)
    pieces = reshape_all(pieces, (fields, half_width, plane_cells))
    k_index = jnp.arange(half_width, dtype=jnp.int32)
    x_index = jnp.arange(x_cells, dtype=jnp.int32)
    angles = phase_of(k_index[:, None] * x_index[None, :], x_cells)
    weight = jnp.where(k_index == 0, 1.0, 2.0).astype(jnp.float32)[:, None]
    real_out = jnp.einsum("fkm,kx->fmx", pieces[0], weight * jnp.cos(angles), precision=HIGHEST)
    imag_out = jnp.einsum("fkm,kx->fmx", pieces[1], weight * jnp.sin(angles), precision=HIGHEST)
    return (real_out - imag_out).reshape(fields, z_cells, y_cells, x_cells)


def spectral_tables(z_cells, y_cells, x_cells):
    row_count = lax.axis_size("row")
    col_count = lax.axis_size("col")
    block_share = row_count // col_count
    per_row = x_cells // 2 // row_count
    plane = jnp.arange(z_cells * y_cells, dtype=jnp.int32)
    z_wave = (
        jnp.arange(col_count, dtype=jnp.int32)[:, None, None, None]
        + col_count * (plane // y_cells)[None, None, None, :]
    )
    y_wave = (lax.axis_index("col") * block_share + jnp.arange(block_share, dtype=jnp.int32))[
        None, :, None, None
    ] + row_count * (plane % y_cells)[None, None, None, :]
    x_wave = (lax.axis_index("row") * per_row + jnp.arange(per_row, dtype=jnp.int32))[
        None, None, :, None
    ]
    k_extent = (col_count, block_share, per_row, z_cells * y_cells)
    angle_list = [
        jnp.broadcast_to(member, k_extent)
        for member in (
            phase_of(x_wave, x_cells),
            phase_of(y_wave, row_count * y_cells),
            phase_of(z_wave, col_count * z_cells),
        )
    ]
    plus_symbols = [(jnp.cos(member) - 1.0, jnp.sin(member)) for member in angle_list]
    minus_symbols = [(1.0 - jnp.cos(member), jnp.sin(member)) for member in angle_list]
    spread = (
        4.0 * jnp.sin(0.5 * angle_list[0]) ** 2
        + 4.0 * jnp.sin(0.5 * angle_list[1]) ** 2
        + 4.0 * jnp.sin(0.5 * angle_list[2]) ** 2
    )
    zero_mode = (x_wave == 0) & (y_wave == 0) & (z_wave == 0)
    total_cells = float(x_cells * row_count * y_cells * col_count * z_cells)
    multiplier = jnp.where(
        zero_mode,
        0.0,
        1.0 / (REFERENCE_DIFFUSIVITY * jnp.where(zero_mode, 1.0, spread) * total_cells),
    )
    return (plus_symbols, minus_symbols, multiplier)


def times_symbol(symbol, pieces):
    symbol_real, symbol_imag = symbol
    return (
        symbol_real * pieces[0] - symbol_imag * pieces[1],
        symbol_real * pieces[1] + symbol_imag * pieces[0],
    )


def stack_symbols(symbols, pieces):
    products = [times_symbol(symbol, pieces) for symbol in symbols]
    return (
        jnp.concatenate([member[0] for member in products], axis=0),
        jnp.concatenate([member[1] for member in products], axis=0),
    )


def contract_symbols(symbols, pieces):
    real_sum = jnp.zeros_like(pieces[0][0:1])
    imag_sum = jnp.zeros_like(pieces[1][0:1])
    for direction in range(3):
        product = times_symbol(
            symbols[direction],
            (pieces[0][direction : direction + 1], pieces[1][direction : direction + 1]),
        )
        real_sum = real_sum + product[0]
        imag_sum = imag_sum + product[1]
    return (real_sum, imag_sum)


def rescale(multiplier, pieces):
    return (multiplier * pieces[0], multiplier * pieces[1])


def on_device_general(volume):
    z_cells, y_cells, x_cells = volume.shape
    smooth = volume
    for sweep_index in range(PASSES):
        padded = with_halo(smooth, (("row", 1), ("col", 0)), 1)
        smooth = diffuse(padded)
    diffusivity = LOW_DIFFUSIVITY + DIFFUSIVITY_SPAN * jax.nn.sigmoid(GRAY_SLOPE * smooth)
    excess = diffusivity - REFERENCE_DIFFUSIVITY
    plus_symbols, minus_symbols, multiplier = spectral_tables(z_cells, y_cells, x_cells)
    source = (excess - jnp.roll(excess, 1, axis=2))[None]
    potential_hat = rescale(multiplier, forward(source))
    unit_load = jnp.array([1.0, 0.0, 0.0], jnp.float32)[:, None, None, None]
    gradients = inverse(stack_symbols(plus_symbols, potential_hat), z_cells, y_cells, x_cells)
    tau_hat = forward(excess[None] * (gradients + unit_load))
    potential_hat = rescale(multiplier, contract_symbols(minus_symbols, tau_hat))
    gradient_x = inverse(times_symbol(plus_symbols[0], potential_hat), z_cells, y_cells, x_cells)[0]
    flux_x = diffusivity * (1.0 + gradient_x)
    return (smooth, flux_x)


MESH = pl.DeviceIdType.MESH
NT = (((1,), (1,)), ((), ()))
NN = (((1,), (0,)), ((), ()))
LANES = 128
SUBLANES = 8
HALVES = 2
QUADS = 4
EXCHANGES = PASSES + 1


def split(values):
    high = values.astype(jnp.bfloat16)
    return high, (values - high.astype(jnp.float32)).astype(jnp.bfloat16)


def split_numpy(values):
    high = values.astype(np.float32).astype(jnp.bfloat16)
    return high, (values - high.astype(np.float64)).astype(np.float32).astype(jnp.bfloat16)


def host_tables(rows, cols, z_cells, y_cells, x_cells):
    devices = rows * cols
    waves = x_cells // 2
    k = np.arange(waves)
    turn = 2.0 * np.pi * ((k[:, None] * np.arange(x_cells)[None, :]) % x_cells) / x_cells
    wave = np.stack([np.cos(turn), -np.sin(turn)])
    wave = wave.reshape(2, devices, HALVES, QUADS, x_cells).transpose(2, 1, 0, 3, 4)
    wave = wave.reshape(2 * waves, x_cells)
    zl, yl = np.divmod(np.arange(LANES), y_cells)
    c, r = np.divmod(np.arange(devices), rows)
    inner = 2.0 * np.pi * (zl[:, None] * zl[None, :] / z_cells + yl[:, None] * yl[None, :] / y_cells)
    cosine, sine = np.cos(inner), np.sin(inner)
    plane = np.concatenate([cosine, sine], axis=1)
    nz, ny = cols * z_cells, rows * y_cells
    twist = 2.0 * np.pi * (c[:, None] * zl[None, :] / nz + r[:, None] * yl[None, :] / ny)
    kz = c[:, None] + cols * zl[None, :]
    ky = r[:, None] + rows * yl[None, :]
    lam_zy = 4.0 * np.sin(np.pi * kz / nz) ** 2 + 4.0 * np.sin(np.pi * ky / ny) ** 2
    lam_x = 4.0 * np.sin(np.pi * k / x_cells) ** 2
    weight = np.where(k == 0, 1.0, 2.0) / (REFERENCE_DIFFUSIVITY * nz * ny * x_cells)
    shape = (devices, SUBLANES, LANES)
    sign = np.where(np.arange(SUBLANES) < QUADS, 1.0, -1.0)[None, :, None]
    members = [np.cos(twist)[:, None, :], np.sin(twist)[:, None, :] * sign, lam_zy[:, None, :]]
    for member in (lam_x, weight):
        member = member.reshape(devices, HALVES, 1, QUADS)
        member = np.broadcast_to(member, (devices, HALVES, 2, QUADS))
        for half in range(HALVES):
            members.append(member[:, half].reshape(devices, SUBLANES, 1))
    small = np.stack([np.broadcast_to(m, shape) for m in members]).astype(np.float32)
    return split_numpy(wave) + split_numpy(plane) + (small,)


def small_fft(items, sign, turned):
    size = len(items)
    if size == 1:
        return items
    even, odd = small_fft(items[::2], sign, turned), small_fft(items[1::2], sign, turned)
    low, high = [], []
    for k in range(size // 2):
        item = odd[k]
        if 4 * k == size:
            item = -sign * turned(item)
        elif k:
            angle = 2 * math.pi * k / size
            item = math.cos(angle) * item - (sign * math.sin(angle)) * turned(item)
        low.append(even[k] + item)
        high.append(even[k] - item)
    return low + high


def grid_fft(items, rows, cols, sign, turned):
    lines = [small_fft(items[c * rows : (c + 1) * rows], sign, turned) for c in range(cols)]
    columns = [small_fft([lines[c][r] for c in range(cols)], sign, turned) for r in range(rows)]
    return [columns[r][c] for c in range(cols) for r in range(rows)]


def kernel(
    rows, cols, z_cells, y_cells, x_cells,
    volume, wave_hi_hbm, wave_lo_hbm, plane_hi_hbm, plane_lo_hbm, small_hbm,
    smooth_out, flux_out,
    wave_hi, wave_lo, plane_hi, plane_lo, small,
    field, excess_ref, y_send, y_recv, z_recv, ey_send, ey_recv, ez_recv,
    packed, arrived,
    table_sem, halo_send, halo_recv, e_send, e_recv, all_send, all_recv,
):
    devices = rows * cols
    cells = z_cells * y_cells
    row, col = lax.axis_index("row"), lax.axis_index("col")
    me = col * rows + row
    up_row, down_row = lax.rem(row + 1, rows), lax.rem(row + rows - 1, rows)
    up_col, down_col = lax.rem(col + 1, cols), lax.rem(col + cols - 1, cols)

    loads = [
        pltpu.make_async_copy(source, target, table_sem.at[i])
        for i, (source, target) in enumerate(
            (
                (wave_hi_hbm, wave_hi), (wave_lo_hbm, wave_lo), (plane_hi_hbm, plane_hi),
                (plane_lo_hbm, plane_lo), (small_hbm, small), (volume, field.at[0]),
            )
        )
    ]
    for load in loads:
        load.start()

    barrier = pltpu.get_barrier_semaphore()

    def greet(step, carry):
        other = lax.rem(me + step, devices)
        pl.semaphore_signal(
            barrier, inc=1, device_id=(lax.rem(other, rows), other // rows), device_id_type=MESH
        )
        return carry

    lax.fori_loop(1, devices, greet, 0)
    pl.semaphore_wait(barrier, devices - 1)

    place = lax.broadcasted_iota(jnp.int32, (cells, x_cells), 0)
    first_y = lax.rem(place, y_cells) == 0
    last_y = lax.rem(place, y_cells) == y_cells - 1

    def spread(edge):
        wide = jnp.broadcast_to(edge[:, None, :], (z_cells, y_cells, x_cells))
        return wide.reshape(cells, x_cells)

    def edge_of(values, y):
        return values.reshape(z_cells, y_cells, x_cells)[:, y, :]

    def remote(source, target, send, recv, device):
        return pltpu.make_async_remote_copy(
            src_ref=source, dst_ref=target, send_sem=send, recv_sem=recv,
            device_id=device, device_id_type=MESH,
        )

    def start_halo(e):
        y_send[e, 0] = edge_of(field[e], y_cells - 1)
        y_send[e, 1] = edge_of(field[e], 0)
        copies = (
            remote(y_send.at[e, 0], y_recv.at[e, 0], halo_send.at[e, 0], halo_recv.at[e, 0], (up_row, col)),
            remote(y_send.at[e, 1], y_recv.at[e, 1], halo_send.at[e, 1], halo_recv.at[e, 1], (down_row, col)),
            remote(field.at[e, pl.ds(cells - y_cells, y_cells)], z_recv.at[e, 0],
                   halo_send.at[e, 2], halo_recv.at[e, 2], (row, up_col)),
            remote(field.at[e, pl.ds(0, y_cells)], z_recv.at[e, 1],
                   halo_send.at[e, 3], halo_recv.at[e, 3], (row, down_col)),
        )
        for copy in copies:
            copy.start()
        return copies

    def next_x(v):
        return pltpu.roll(v, x_cells - 1, 1)

    def prev_x(v):
        return pltpu.roll(v, 1, 1)

    def limited(differ):
        scaled = differ / EDGE_SCALE
        return differ / (1.0 + scaled * scaled)

    def between(flow):
        none = jnp.zeros((y_cells, x_cells), jnp.float32)
        return jnp.concatenate([flow, none], axis=0) - jnp.concatenate([none, flow], axis=0)

    def z_ends(low, high):
        none = jnp.zeros((cells - 2 * y_cells, x_cells), jnp.float32)
        return jnp.concatenate([-low, none, high], axis=0)

    def y_ends(low, high):
        return jnp.where(last_y, spread(high), jnp.where(first_y, -spread(low), 0.0))

    pending = []
    loads.pop().wait()
    for sweep in range(PASSES):
        copies = start_halo(sweep)
        pending += copies
        now = field[sweep]
        flow = limited(next_x(now) - now)
        total = flow - prev_x(flow)
        flow = jnp.where(last_y, 0.0, limited(pltpu.roll(now, cells - 1, 0) - now))
        total = total + (flow - pltpu.roll(flow, 1, 0))
        flow = limited(now[y_cells:] - now[:-y_cells])
        total = total + between(flow)
        copies[2].wait_recv()
        copies[3].wait_recv()
        z_low = limited(now[:y_cells] - z_recv[sweep, 0])
        z_high = limited(z_recv[sweep, 1] - now[-y_cells:])
        total = total + z_ends(z_low, z_high)
        copies[0].wait_recv()
        copies[1].wait_recv()
        y_low = limited(edge_of(now, 0) - y_recv[sweep, 0])
        y_high = limited(y_recv[sweep, 1] - edge_of(now, y_cells - 1))
        total = total + y_ends(y_low, y_high)
        later = now + TIME_STEP * total
        if sweep < PASSES - 1:
            field[sweep + 1] = later
    smooth_out[...] = later.reshape(z_cells, y_cells, x_cells)
    diffusivity = LOW_DIFFUSIVITY + DIFFUSIVITY_SPAN / (1.0 + jnp.exp(-GRAY_SLOPE * later))
    flux_out[...] = diffusivity.reshape(z_cells, y_cells, x_cells)
    excess = diffusivity - REFERENCE_DIFFUSIVITY
    excess_ref[...] = excess
    ey_send[...] = edge_of(excess, y_cells - 1)
    e_copies = (
        remote(ey_send, ey_recv, e_send.at[0], e_recv.at[0], (up_row, col)),
        remote(excess_ref.at[pl.ds(cells - y_cells, y_cells)], ez_recv, e_send.at[1], e_recv.at[1], (row, up_col)),
    )
    for copy in e_copies:
        copy.start()
    pending += e_copies
    for load in loads:
        load.wait()

    def start_exchange(turn, half):
        def send(step, carry):
            to_row = lax.rem(row + step // cols, rows)
            to_col = lax.rem(col + step, cols)
            remote(
                packed.at[turn, half, to_col * rows + to_row], arrived.at[turn, half, me],
                all_send.at[turn, half], all_recv.at[turn, half], (to_row, to_col),
            ).start()
            return carry

        lax.fori_loop(1, devices, send, 0)
        arrived[turn, half, me] = packed[turn, half, me]

    def end_exchange(turn, half):
        block = arrived.at[turn, half, pl.ds(0, devices - 1)]
        pltpu.make_async_copy(block, block, all_recv.at[turn, half]).wait()

    def finish(turn, half):
        block = packed.at[turn, half, pl.ds(0, devices - 1)]
        pltpu.make_async_copy(block, block, all_send.at[turn, half]).wait()

    real_rows = lax.broadcasted_iota(jnp.int32, (SUBLANES, LANES), 0) < QUADS

    def swapped(tile):
        return pltpu.roll(tile, QUADS, 0)

    def turned(tile):
        tile = swapped(tile)
        return jnp.where(real_rows, tile, -tile)

    def product(a, b, dims):
        return lax.dot_general(a, b, dims, preferred_element_type=jnp.float32)

    def row_product(values, high, low, dims):
        values_hi, values_lo = split(values)
        count = values.shape[0]
        both = product(jnp.concatenate([values_hi, values_lo], axis=0), high, dims)
        return both[:count] + (both[count:] + product(values_hi, low, dims))

    many = devices * SUBLANES
    side = lax.rem(lax.broadcasted_iota(jnp.int32, (many, LANES), 0), SUBLANES) < QUADS

    def plane_product(values, sign):
        both = row_product(values, plane_hi[...], plane_lo[...], NN)
        cosine, sine = both[:, :LANES], both[:, LANES:]
        sine = jnp.where(side, pltpu.roll(sine, many - QUADS, 0), -pltpu.roll(sine, QUADS, 0))
        return cosine - sign * sine

    def spectral(turn, half):
        items = [arrived[turn, half, d] for d in range(devices)]
        items = grid_fft(items, rows, cols, -1.0, turned)
        items = [t * small[0, d] + swapped(t) * small[1, d] for d, t in enumerate(items)]
        waves = plane_product(jnp.concatenate(items, axis=0), -1.0)
        lam = small[2] + small[3 + half, me][None]
        weight = small[3 + HALVES + half, me][None]
        factor = jnp.where(lam == 0.0, 0.0, weight / jnp.where(lam == 0.0, 1.0, lam))
        waves = plane_product(waves * factor.reshape(many, LANES), 1.0)
        items = [waves[d * SUBLANES : (d + 1) * SUBLANES] for d in range(devices)]
        items = [t * small[0, d] - swapped(t) * small[1, d] for d, t in enumerate(items)]
        for d, t in enumerate(grid_fft(items, rows, cols, 1.0, turned)):
            packed[turn + 1, half, d] = t

    def solve(source, turn):
        source_hi, source_lo = split(source)
        sources = jnp.concatenate([source_hi, source_lo], axis=0)
        for half in range(HALVES):
            part = pl.ds(half * many, many)
            both = product(wave_hi[part, :], sources, NT)
            spectrum = both[:, :cells] + (
                both[:, cells:] + product(wave_lo[part, :], source_hi, NT)
            )
            packed[turn, half] = spectrum.reshape(devices, SUBLANES, LANES)
            start_exchange(turn, half)
        for half in range(HALVES):
            end_exchange(turn, half)
            spectral(turn, half)
            start_exchange(turn + 1, half)
        total = None
        for half in range(HALVES):
            part = pl.ds(half * many, many)
            end_exchange(turn + 1, half)
            back = arrived[turn + 1, half].reshape(many, LANES)
            piece = row_product(back.T, wave_hi[part, :], wave_lo[part, :], NN)
            total = piece if half == 0 else total + piece
        return total

    potential = solve(excess - prev_x(excess), 0)
    field[PASSES] = potential
    copies = start_halo(PASSES)
    pending += copies
    potential = field[PASSES]
    excess = excess_ref[...]
    tau = excess * (1.0 + (next_x(potential) - potential))
    diverge = tau - prev_x(tau)
    tau = excess * jnp.where(last_y, 0.0, pltpu.roll(potential, cells - 1, 0) - potential)
    diverge = diverge + (tau - pltpu.roll(tau, 1, 0))
    diverge = diverge + between(excess[:-y_cells] * (potential[y_cells:] - potential[:-y_cells]))
    for copy in e_copies + copies[2:]:
        copy.wait_recv()
    z_low = ez_recv[...] * (potential[:y_cells] - z_recv[PASSES, 0])
    z_high = excess[-y_cells:] * (z_recv[PASSES, 1] - potential[-y_cells:])
    diverge = diverge + z_ends(z_low, z_high)
    for copy in copies[:2]:
        copy.wait_recv()
    y_low = ey_recv[...] * (edge_of(potential, 0) - y_recv[PASSES, 0])
    y_high = edge_of(excess, y_cells - 1) * (
        y_recv[PASSES, 1] - edge_of(potential, y_cells - 1)
    )
    diverge = diverge + y_ends(y_low, y_high)
    potential = solve(diverge, 2)
    gradient = next_x(potential) - potential
    flux_out[...] = flux_out[...] * (1.0 + gradient.reshape(z_cells, y_cells, x_cells))
    for copy in pending:
        copy.wait_send()
    for turn in range(4):
        for half in range(HALVES):
            finish(turn, half)


def on_device(rows, cols, tables, volume):
    z_cells, y_cells, x_cells = volume.shape
    devices, cells = rows * cols, z_cells * y_cells
    f32, bf16 = jnp.float32, jnp.bfloat16
    vmem = pl.BlockSpec(memory_space=pltpu.VMEM)
    scratch = [pltpu.VMEM(table.shape, table.dtype) for table in tables] + [
        pltpu.VMEM((EXCHANGES, cells, x_cells), f32),
        pltpu.VMEM((cells, x_cells), f32),
        pltpu.VMEM((EXCHANGES, 2, z_cells, x_cells), f32),
        pltpu.VMEM((EXCHANGES, 2, z_cells, x_cells), f32),
        pltpu.VMEM((EXCHANGES, 2, y_cells, x_cells), f32),
        pltpu.VMEM((z_cells, x_cells), f32),
        pltpu.VMEM((z_cells, x_cells), f32),
        pltpu.VMEM((y_cells, x_cells), f32),
        pltpu.VMEM((4, HALVES, devices, SUBLANES, LANES), f32),
        pltpu.VMEM((4, HALVES, devices, SUBLANES, LANES), f32),
        pltpu.SemaphoreType.DMA((len(tables) + 1,)),
        pltpu.SemaphoreType.DMA((EXCHANGES, 4)),
        pltpu.SemaphoreType.DMA((EXCHANGES, 4)),
        pltpu.SemaphoreType.DMA((2,)),
        pltpu.SemaphoreType.DMA((2,)),
        pltpu.SemaphoreType.DMA((4, HALVES)),
        pltpu.SemaphoreType.DMA((4, HALVES)),
    ]
    shape = jax.ShapeDtypeStruct(volume.shape, f32)
    return pl.pallas_call(
        functools.partial(kernel, rows, cols, z_cells, y_cells, x_cells),
        out_shape=(shape, shape),
        in_specs=[pl.BlockSpec(memory_space=pl.ANY)] * (len(tables) + 1),
        out_specs=(vmem, vmem),
        scratch_shapes=scratch,
        compiler_params=pltpu.CompilerParams(
            collective_id=0, has_side_effects=True, vmem_limit_bytes=60 * 1024 * 1024
        ),
    )(volume.reshape(cells, x_cells), *tables)


def power_of_two(count):
    return count & (count - 1) == 0


def block_function(rows, cols, volume):
    z_cells, y_cells, x_cells = volume.shape
    devices = rows * cols
    direct = (
        x_cells // 2 == SUBLANES * devices
        and z_cells * y_cells == LANES
        and z_cells % 8 == 0
        and y_cells % 8 == 0
        and power_of_two(rows)
        and power_of_two(cols)
        and min(rows, cols) > 2
    )
    if not direct:
        return on_device_general(volume)
    tables = [jnp.asarray(t) for t in host_tables(rows, cols, z_cells, y_cells, x_cells)]
    return on_device(rows, cols, tables, volume)


def solution(mesh):
    return jax.shard_map(
        functools.partial(block_function, mesh.shape["row"], mesh.shape["col"]),
        mesh=mesh,
        in_specs=(P("col", "row", None),),
        out_specs=(P("col", "row", None), P("col", "row", None)),
        check_vma=False,
    )
```
